32 devices in a mesh: seq: 4 (over x, core), batch: 8 (over z, y).
Axes of the slice: x: 2, y: 2, z: 4, core: 2. Of those that a mesh axis runs over, the one named last changes fastest.
Arguments:
- hidden: bfloat16 [4096, 512], P(('batch', 'seq')), parts along dimension 0, may hold values from -500 to 500
- norm_gain: float32 [512], replicated, may hold values from 0.5 to 1.5
- input_weight: bfloat16 [512, 2176], replicated, may hold values from -0.25 to 0.25
- step_weight: bfloat16 [512, 16], replicated, may hold values from -1 to 1
- conv_weight: float32 [4, 1152], replicated, may hold values from -3 to 3
- conv_bias: float32 [1152], replicated, may hold values from -3 to 3
- step_bias: float32 [16], replicated, may hold values from -11 to 1
- log_rate: float32 [16], replicated, may hold values from -3 to 6
- skip_gain: float32 [16], replicated, may hold values from 0.5 to 1.5
- gate_gain: float32 [1024], replicated, may hold values from 0.5 to 1.5
- output_weight: bfloat16 [1024, 512], replicated, may hold values from -0.1875 to 0.1875
Outputs:
- mixed: bfloat16 [4096, 512], P(('batch', 'seq')), parts along dimension 0
The draws below stay inside these ranges and needn't reach their ends.
There are 8 independent parts, one for each index of `batch`. The reference program is written for one: setup_inputs(seed, part) draws one part's arguments, and reference() takes and returns one part's arrays. A program takes and returns all parts, laid end to end along the dimension named above; an argument that names none is the same for every part. Nothing has to cross between parts.
All inputs are finite; a program needn't handle non-finite values.
Results may differ from the reference program's by a relative error of at most 0.0078.
Values may be sent and summed in bfloat16 or wider, within the bound.
No kernel may reach another device: no remote copies, remote signals or barrier semaphores. Data moves between devices by JAX's collectives and lax.ppermute only.
A program may use at most 128 MiB of HBM per device.

```python
import math
import jax
import jax.numpy as jnp
from jax import lax

EMBED_DIM = 512
E = 1024
N = 64
P_SIZE = 64
K = 4
BLOCK = 128
HEADS = 16
TOKEN_COUNT = 512


def polarity_pattern(feature_count):
    index_row = jnp.arange(feature_count)
    return jnp.where((index_row * 7919 + 13) % 29 < 14, 1.0, -1.0).astype(jnp.float32)


def draw_hidden(key, part):
    prng_seeds = jax.random.split(key, 4)
    drawn_input = jnp.clip(jax.random.normal(prng_seeds[0], (TOKEN_COUNT, EMBED_DIM), jnp.float32), -5.0, 5.0)
    token_multiplier = jnp.exp(jax.random.uniform(prng_seeds[1], (TOKEN_COUNT, 1), jnp.float32) * math.log(10.0))
    channel_multiplier = jnp.exp(jax.random.uniform(prng_seeds[2], (1, EMBED_DIM), jnp.float32) * math.log(10.0))
    spike_input = jax.random.randint(prng_seeds[3], (TOKEN_COUNT, 1), 0, TOKEN_COUNT) < 4
    entry_matrix = jnp.where(spike_input, 8.0 * polarity_pattern(EMBED_DIM)[None, :] + 0.3 * drawn_input, token_multiplier * channel_multiplier * drawn_input)
    return entry_matrix.astype(jnp.bfloat16)


def draw_step_weight(key, part):
    noise = jax.random.normal(key, (EMBED_DIM, HEADS), jnp.float32) / math.sqrt(EMBED_DIM)
    aligned = (math.log(TOKEN_COUNT) + 3.0) * polarity_pattern(EMBED_DIM)[:, None] / EMBED_DIM
    return jnp.clip(noise + aligned, -1.0, 1.0).astype(jnp.bfloat16)


def draw_step_bias(key, part):
    offset = jax.random.uniform(key, (HEADS,), jnp.float32, 0.0, 1.0)
    return (offset - math.log(TOKEN_COUNT)).astype(jnp.float32)


def draw_log_rate(key, part):
    prng_seeds = jax.random.split(key, 3)
    order = jax.random.permutation(prng_seeds[0], HEADS)
    slow = order < HEADS // 2
    slow_value = jax.random.uniform(prng_seeds[1], (HEADS,), jnp.float32, math.log(0.07), math.log(0.25))
    fast_value = jax.random.uniform(prng_seeds[2], (HEADS,), jnp.float32, 0.0, math.log(max(0.013 * TOKEN_COUNT, 2.0)))
    return jnp.where(slow, slow_value, fast_value).astype(jnp.float32)


def bell_draw(stream_key, dims, width, limit, dtype=jnp.bfloat16):
    entries = jax.random.normal(stream_key, dims, jnp.float32) * width
    return jnp.minimum(jnp.maximum(entries, -limit), limit).astype(dtype)


def setup_inputs(seed: int = 0, part: int = 0) -> dict:
    streams_of = jax.random.split(jax.random.key(seed), 12)
    part_splits = jax.random.split(jax.random.fold_in(streams_of[11], part), 12)
    hidden = draw_hidden(jax.random.fold_in(jax.random.fold_in(streams_of[11], part), 71), part)
    norm_gain = jnp.clip(1.0 + 0.1 * jax.random.normal(streams_of[1], (EMBED_DIM,), jnp.float32), 0.5, 1.5)
    input_weight = bell_draw(streams_of[2], (EMBED_DIM, 2 * E + 2 * N), EMBED_DIM ** -0.5, 0.25)
    step_weight = draw_step_weight(jax.random.fold_in(streams_of[11], 71), part)
    conv_weight = bell_draw(streams_of[4], (K, E + 2 * N), K ** -0.5, 3.0, jnp.float32)
    conv_bias = bell_draw(streams_of[5], (E + 2 * N,), 0.5, 3.0, jnp.float32)
    step_bias = draw_step_bias(jax.random.fold_in(streams_of[11], 71), part)
    log_rate = draw_log_rate(jax.random.fold_in(streams_of[11], 71), part)
    skip_gain = jnp.clip(jax.random.uniform(streams_of[8], (HEADS,), jnp.float32, 0.5, 1.5), 0.5, 1.5)
    gate_gain = jnp.clip(1.0 + 0.1 * jax.random.normal(streams_of[9], (E,), jnp.float32), 0.5, 1.5)
    output_weight = bell_draw(streams_of[10], (E, EMBED_DIM), E ** -0.5, 0.1875)
    return dict(hidden=hidden, norm_gain=norm_gain, input_weight=input_weight, step_weight=step_weight, conv_weight=conv_weight, conv_bias=conv_bias, step_bias=step_bias, log_rate=log_rate, skip_gain=skip_gain, gate_gain=gate_gain, output_weight=output_weight)


eps = 1e-05

def normed(entry_matrix, gain):
    floats = entry_matrix.astype(jnp.float32)
    scale = lax.rsqrt(lax.optimization_barrier(jnp.mean(floats * floats, axis=-1, keepdims=True)) + eps)
    return (floats * scale * gain).astype(jnp.bfloat16)

def block_step(memory, pieces):
    signal, writer, reader, log_decay = pieces
    cumulated = jnp.cumsum(log_decay, axis=0)
    per_head = cumulated.T
    spread = per_head[:, :, None] - per_head[:, None, :]
    causal = lax.broadcasted_iota(jnp.int32, (BLOCK, BLOCK), 0) >= lax.broadcasted_iota(jnp.int32, (BLOCK, BLOCK), 1)
    decay = jnp.where(causal[None], jnp.exp(jnp.where(causal[None], spread, 0.0)), 0.0)
    scores = jnp.dot(reader, writer.T, preferred_element_type=jnp.float32)
    weights = (decay * scores[None]).astype(jnp.bfloat16)
    heads_x = signal.reshape(BLOCK, HEADS, P_SIZE)
    inside = jnp.einsum('hts,shp->thp', weights.astype(jnp.float32), heads_x.astype(jnp.float32))
    carried = jnp.einsum('tn,hnp->thp', reader.astype(jnp.float32), memory, precision=lax.Precision.HIGHEST)
    result = inside + jnp.exp(cumulated)[:, :, None] * carried
    decay_tail = jnp.exp(cumulated[-1][None, :] - cumulated)
    decayed = (decay_tail[:, :, None] * heads_x.astype(jnp.float32)).astype(jnp.bfloat16)
    renewed = jnp.exp(cumulated[-1])[:, None, None] * memory + jnp.einsum('sn,shp->hnp', writer.astype(jnp.float32), decayed.astype(jnp.float32))
    return (renewed, result.reshape(BLOCK, E))

def reference(hidden, norm_gain, input_weight, step_weight, conv_weight, conv_bias, step_bias, log_rate, skip_gain, gate_gain, output_weight):

    def mixer(sequence):
        normal_rows = normed(sequence, norm_gain)
        projected = jnp.dot(normal_rows, input_weight, preferred_element_type=jnp.float32).astype(jnp.bfloat16)
        step_raw = jnp.dot(normal_rows, step_weight, preferred_element_type=jnp.float32)
        extended = jnp.concatenate([jnp.zeros((K - 1, E + 2 * N), jnp.bfloat16), projected[:, E:]], axis=0)
        filtered = conv_bias[None, :]
        for tap_index in range(K):
            filtered = filtered + conv_weight[tap_index][None, :] * extended[tap_index:tap_index + TOKEN_COUNT].astype(jnp.float32)
        activated = jax.nn.silu(filtered).astype(jnp.bfloat16)
        signal = activated[:, :E]
        writer = activated[:, E:E + N]
        reader = activated[:, E + N:]
        log_decay = -jnp.exp(log_rate)[None, :] * jax.nn.softplus(step_raw + step_bias[None, :])
        blocks = TOKEN_COUNT // BLOCK
        start = jnp.zeros((HEADS, N, P_SIZE), jnp.float32)
        final_memory, inside = lax.scan(block_step, start, (signal.reshape(blocks, BLOCK, E), writer.reshape(blocks, BLOCK, N), reader.reshape(blocks, BLOCK, N), log_decay.reshape(blocks, BLOCK, HEADS)))
        output_rows = inside.reshape(TOKEN_COUNT, E)
        gated = (output_rows + jnp.repeat(skip_gain, P_SIZE)[None, :] * signal.astype(jnp.float32)) * jax.nn.silu(projected[:, :E].astype(jnp.float32))
        return jnp.dot(normed(gated, gate_gain), output_weight, preferred_element_type=jnp.float32)
    first_chain = mixer(hidden)
    second_chain = mixer(hidden[:, ::-1])
    third_chain = mixer(hidden[::-1])
    fourth_chain = mixer(hidden[::-1, ::-1])
    forward_part = first_chain + second_chain[:, ::-1]
    backward_part = (third_chain + fourth_chain[:, ::-1])[::-1].astype(jnp.bfloat16)
    backward_part = lax.optimization_barrier(backward_part)
    return (forward_part + backward_part.astype(jnp.float32)).astype(jnp.bfloat16)
```

```python
import functools

import jax
import jax.numpy as jnp
from jax import lax
from jax.experimental import pallas as pl
from jax.experimental.pallas import tpu as pltpu
from jax.sharding import PartitionSpec as P

EMBED = 512
E = 1024
N = 64
K = 4
BLOCK = 128
HEADS = 16
MIXED = E + 2 * N
TILES = MIXED // 128
PAIRS = E // 128
GROUPS = EMBED // 128
PAD = 8
EDGE = 16
eps = 1e-05
F32 = jnp.float32
BF16 = jnp.bfloat16


def dot(a, b):
    return jnp.dot(a, b, preferred_element_type=F32)


def iota(shape, axis):
    return lax.broadcasted_iota(jnp.int32, shape, axis)


def reversal():
    return (iota((128, 128), 0) + iota((128, 128), 1) == 127).astype(BF16)


def split(values, terms):
    parts = []
    for _ in range(terms):
        part = values.astype(BF16)
        parts.append(part)
        values = values - part.astype(F32)
    return parts


def exact_dot(mask, values):
    return sum(dot(mask, part) for part in split(values, 3))


def flip_lanes(rows, swap):
    return jnp.concatenate(
        [dot(rows[:, 128 * (GROUPS - 1 - g) : 128 * (GROUPS - g)], swap) for g in range(GROUPS)],
        axis=1,
    )


def both_normed(rows, gain, swap):
    floats = rows.astype(F32)
    scale = lax.rsqrt(jnp.mean(floats * floats, axis=-1, keepdims=True) + eps)
    flipped = flip_lanes(rows.astype(BF16), swap)
    return [(floats * scale * gain).astype(BF16), (flipped * scale * gain).astype(BF16)]


def half_silu(half):
    return half + half * jnp.tanh(half)


def log_decays(step_raw, step_bias, log_rate):
    v = step_raw + step_bias
    return -jnp.exp(log_rate) * (jnp.maximum(v, 0.0) + jnp.log1p(jnp.exp(-jnp.abs(v))))


def pad_lanes(values):
    return jnp.concatenate(
        [values, jnp.zeros((values.shape[0], 128 - values.shape[1]), F32)], axis=1
    )


def spread_pair(values, pair):
    index = 2 * pair + (iota(values.shape, 1) >= N).astype(jnp.int32)
    return jnp.take_along_axis(values, index, axis=1)


def own_kernel(
    x_ref,
    norm_gain_ref,
    input_weight_ref,
    step_weight_ref,
    conv_weight_ref,
    conv_bias_ref,
    step_bias_ref,
    log_rate_ref,
    activated_ref,
    edge_ref,
    silu_gate_ref,
    decay_ref,
    lift_ref,
    extended_ref,
):
    swap = reversal()
    normal = jnp.concatenate(both_normed(x_ref[...], norm_gain_ref[...], swap), axis=0)

    step_raw = dot(normal, step_weight_ref[...])
    log_decay = log_decays(step_raw, step_bias_ref[...], log_rate_ref[...])
    row, column = iota((2 * BLOCK, 2 * BLOCK), 0), iota((2 * BLOCK, 2 * BLOCK), 1)
    same = (row >= BLOCK) == (column >= BLOCK)
    before = exact_dot((same & (column <= row)).astype(BF16), log_decay)
    after = exact_dot((same & (column >= row)).astype(BF16), log_decay)

    for start in range(0, E, 256):
        gate = dot(normal, input_weight_ref[:, start : start + 256]).astype(BF16).astype(F32)
        gate = half_silu(0.5 * gate)
        for flip in range(2):
            silu_gate_ref[flip, :, start : start + 256] = gate[flip * BLOCK : (flip + 1) * BLOCK]

    for flip in range(2):
        for tile in range(TILES):
            extended_ref[flip, tile, :PAD] = jnp.zeros((PAD, 128), F32)
            extended_ref[flip, tile, PAD + BLOCK :] = jnp.zeros((PAD, 128), F32)
    for start in range(0, MIXED, 256):
        stop = min(start + 256, MIXED)
        mixed = dot(normal, input_weight_ref[:, E + start : E + stop]).astype(BF16).astype(F32)
        for flip in range(2):
            rows = mixed[flip * BLOCK : (flip + 1) * BLOCK]
            edge_ref[flip, :EDGE, start:stop] = rows[:EDGE]
            edge_ref[flip, EDGE:, start:stop] = rows[BLOCK - EDGE :]
            for tile in range(start // 128, stop // 128):
                low = tile * 128 - start
                extended_ref[flip, tile, PAD : PAD + BLOCK] = rows[:, low : low + 128]

    taps, bias = 0.5 * conv_weight_ref[...], 0.5 * conv_bias_ref[...]
    for flip in range(2):
        for tile in range(TILES):
            lanes = slice(tile * 128, tile * 128 + 128)
            ahead = bias[:, lanes]
            behind = bias[:, lanes]
            for k in range(K):
                tap = taps[k : k + 1, lanes]
                low = PAD - (K - 1) + k
                ahead = ahead + tap * extended_ref[flip, tile, low : low + BLOCK]
                low = PAD + (K - 1) - k
                behind = behind + tap * extended_ref[flip, tile, low : low + BLOCK]
            activated_ref[2 * flip, :, lanes] = half_silu(ahead).astype(BF16)
            activated_ref[2 * flip + 1, :, lanes] = half_silu(behind).astype(BF16)

    lower = iota((BLOCK, BLOCK), 0) >= iota((BLOCK, BLOCK), 1)
    for flip in range(2):
        rows = slice(flip * BLOCK, (flip + 1) * BLOCK)
        from_start, to_end = before[rows], after[rows]
        from_start_t, to_end_t = pad_lanes(from_start).T, pad_lanes(to_end).T
        for head in range(HEADS):
            at = slice(head, head + 1)
            spread = jnp.where(
                lower,
                from_start[:, at] - from_start_t[at],
                to_end[:, at] - to_end_t[at],
            )
            decay_ref[flip, head] = jnp.exp(spread)
        wide = pad_lanes(from_start), pad_lanes(to_end)
        for pair in range(PAIRS):
            lanes = slice(pair * 128, pair * 128 + 128)
            for way in range(2):
                lift_ref[2 * flip + way, :, lanes] = jnp.exp(spread_pair(wide[way], pair))


def join_kernel(count, *refs):
    received = refs[: count - 1]
    (
        norm_gain_ref,
        input_weight_ref,
        step_weight_ref,
        conv_weight_ref,
        conv_bias_ref,
        step_bias_ref,
        log_rate_ref,
        skip_gain_ref,
        gate_gain_ref,
        output_weight_ref,
        activated_ref,
        edge_ref,
        silu_gate_ref,
        decay_ref,
        lift_ref,
        out_ref,
        stack_ref,
        normal_ref,
        extended_ref,
        halo_ref,
        memory_ref,
        window_ref,
        gated_ref,
    ) = refs[count - 1 :]
    index = lax.axis_index("seq")
    swap = reversal()
    row, column = iota((BLOCK, BLOCK), 0), iota((BLOCK, BLOCK), 1)
    lower, upper = row >= column, row <= column
    taps, bias = 0.5 * conv_weight_ref[...], 0.5 * conv_bias_ref[...]
    left = iota((BLOCK, 128), 1) < N

    for offset in range(1, count):
        stack_ref[offset - 1] = received[offset - 1][...]
    halo_ref[0] = jnp.zeros(halo_ref.shape[1:], F32)
    memory_ref[...] = jnp.zeros(memory_ref.shape, F32)

    def remote(slots):
        for place, slot in enumerate(slots):
            earlier = slot < index
            offset = jnp.where(earlier, index - slot, slot + 1)
            order = jnp.where(earlier, row, 127 - row) == column
            rows = dot(order.astype(BF16), stack_ref[offset - 1])
            for flip, part in enumerate(both_normed(rows, norm_gain_ref[...], swap)):
                normal_ref[place, flip] = part
        total = len(slots) * 2 * BLOCK
        normal = normal_ref[...].reshape(total, EMBED)

        step_raw = dot(normal, step_weight_ref[...])
        log_decay = log_decays(step_raw, step_bias_ref[...], log_rate_ref[...])
        tails, wholes = [], []
        for part in range(2 * len(slots)):
            rows = log_decay[part * BLOCK : (part + 1) * BLOCK]
            tail = exact_dot((column > row).astype(BF16), rows)
            tails.append(pad_lanes(tail))
            wholes.append(pad_lanes(tail[:8] + rows[:8]))

        writers = [None] * (2 * len(slots))
        starts = [E] + list(range(0, E, 256))
        for start in starts:
            stop = min(start + 256, MIXED)
            mixed = dot(normal, input_weight_ref[:, E + start : E + stop])
            mixed = mixed.astype(BF16).astype(F32)
            for place, slot in enumerate(slots):
                keep = jnp.where(slot == index, 0.0, 1.0)
                for flip in range(2):
                    part = 2 * place + flip
                    rows = mixed[part * BLOCK : (part + 1) * BLOCK]
                    acted = []
                    for tile in range(start // 128, stop // 128):
                        low = tile * 128 - start
                        lanes = slice(tile * 128, tile * 128 + 128)
                        extended_ref[part, tile, :PAD] = keep * halo_ref[slot, flip, :, lanes]
                        extended_ref[part, tile, PAD:] = rows[:, low : low + 128]
                        halo_ref[slot + 1, flip, :, lanes] = rows[BLOCK - PAD :, low : low + 128]
                        filtered = bias[:, lanes]
                        for k in range(K):
                            at = PAD - (K - 1) + k
                            filtered = filtered + taps[k : k + 1, lanes] * extended_ref[
                                part, tile, at : at + BLOCK
                            ]
                        acted.append(half_silu(filtered).astype(BF16))
                    if start == E:
                        writers[part] = acted[0][:, :N].T
                        continue
                    decayed, scales = [], []
                    for near, values in enumerate(acted):
                        pair = start // 128 + near
                        scale = jnp.exp(spread_pair(tails[part], pair))
                        decayed.append((scale * values.astype(F32)).astype(BF16))
                        scales.append(jnp.exp(spread_pair(wholes[part], pair))[:1])
                    added = dot(writers[part], jnp.concatenate(decayed, axis=1))
                    side = jnp.where(slot < index, 0, 1)
                    lanes = slice(start, stop)
                    memory_ref[2 * flip + side, :, lanes] = (
                        jnp.concatenate(scales, axis=1) * memory_ref[2 * flip + side, :, lanes]
                        + added
                    )

    if count <= 5:
        if count > 1:
            remote(list(range(count - 1)))
    else:

        @pl.loop(0, count - 1)
        def _(slot):
            remote([slot])

    skip = exact_dot_row(skip_gain_ref[...])
    for flip in range(2):
        for way in range(2):
            chain = 2 * flip + way
            if way == 0:
                window_ref[:PAD] = halo_ref[index, flip]
                window_ref[PAD : PAD + EDGE] = edge_ref[flip, :EDGE]
            else:
                keep = jnp.where(index < count - 1, 1.0, 0.0)
                window_ref[PAD - 8 : PAD - 8 + EDGE] = edge_ref[flip, EDGE:]
                for step in range(K - 1):
                    window_ref[EDGE + step : EDGE + step + 1] = (
                        keep * halo_ref[count - 1, flip, PAD - 1 - step : PAD - step]
                    )
            filtered = bias
            for k in range(K):
                at = PAD - (K - 1) + k if way == 0 else (K - 1) - k
                filtered = filtered + taps[k : k + 1] * window_ref[at : at + EDGE]
            patch = half_silu(filtered).astype(BF16)

            def acted(tile):
                lanes = slice(tile * 128, tile * 128 + 128)
                if way == 0:
                    parts = [patch[:, lanes], activated_ref[chain, EDGE:, lanes]]
                else:
                    parts = [activated_ref[chain, : BLOCK - EDGE, lanes], patch[:, lanes]]
                return jnp.concatenate(parts, axis=0)

            maps = acted(PAIRS)
            writer, reader = maps[:, :N], maps[:, N:]
            scores = lax.dot_general(
                reader, writer, (((1,), (1,)), ((), ())), preferred_element_type=F32
            )
            scores = jnp.where(lower if way == 0 else upper, scores, 0.0)
            squares = jnp.zeros((BLOCK, 128), F32)
            doubled = jnp.concatenate([reader, reader], axis=1)
            for pair in range(PAIRS):
                lanes = slice(pair * 128, pair * 128 + 128)
                signal = acted(pair)
                zeros = jnp.zeros_like(signal)
                signals = jnp.concatenate(
                    [jnp.where(left, signal, zeros), jnp.where(left, zeros, signal)], axis=0
                )
                weights = jnp.concatenate(
                    [
                        (decay_ref[flip, 2 * pair + near] * scores).astype(BF16)
                        for near in range(2)
                    ],
                    axis=1,
                )
                inside = dot(weights, signals)
                memory = jnp.concatenate(split(memory_ref[chain, :, lanes], 2), axis=0)
                carried = dot(doubled, memory)
                inside = inside + lift_ref[chain, :, lanes] * carried
                gated = inside + skip[:, lanes] * signal.astype(F32)
                gated = gated * silu_gate_ref[flip, :, lanes]
                squares = squares + gated * gated
                gated_ref[chain, :, lanes] = gated
            scale = lax.rsqrt(jnp.sum(squares, axis=1, keepdims=True) * (1.0 / E) + eps)
            for pair in range(PAIRS):
                lanes = slice(pair * 128, pair * 128 + 128)
                gated_ref[chain, :, lanes] = (
                    gated_ref[chain, :, lanes] * scale * gate_gain_ref[:, lanes]
                )

    normed = gated_ref[...].astype(BF16).reshape(4 * BLOCK, E)
    made = dot(normed, output_weight_ref[...])
    straight, turned = made[: 2 * BLOCK], made[2 * BLOCK :]
    high, low = split(turned, 2)
    both = straight + flip_lanes(high, swap) + flip_lanes(low, swap)
    backward = both[BLOCK:].astype(BF16).astype(F32)
    out_ref[...] = (both[:BLOCK] + backward).astype(BF16)


def exact_dot_row(row):
    select = (iota((HEADS, E), 1) // N == iota((HEADS, E), 0)).astype(BF16)
    rows = jnp.broadcast_to(row, (8, HEADS))
    return sum(dot(part, select) for part in split(rows, 3))[:1]


def on_device(
    hidden,
    norm_gain,
    input_weight,
    step_weight,
    conv_weight,
    conv_bias,
    step_bias,
    log_rate,
    skip_gain,
    gate_gain,
    output_weight,
):
    count = lax.axis_size("seq")
    received = [
        lax.ppermute(hidden, "seq", [(i, (i + offset) % count) for i in range(count)])
        for offset in range(1, count)
    ]
    row = lambda vector: vector.reshape(1, -1)
    whole = pl.BlockSpec(memory_space=pltpu.VMEM)
    shared = [
        row(norm_gain),
        input_weight,
        step_weight,
        conv_weight,
        row(conv_bias),
        row(step_bias),
        row(log_rate),
    ]
    shape = jax.ShapeDtypeStruct
    own = pl.pallas_call(
        own_kernel,
        out_shape=[
            shape((4, BLOCK, MIXED), BF16),
            shape((2, 2 * EDGE, MIXED), F32),
            shape((2, BLOCK, E), F32),
            shape((2, HEADS, BLOCK, BLOCK), F32),
            shape((4, BLOCK, E), F32),
        ],
        in_specs=[whole] * 8,
        out_specs=[whole] * 5,
        scratch_shapes=[pltpu.VMEM((2, TILES, BLOCK + 2 * PAD, 128), F32)],
        compiler_params=pltpu.CompilerParams(vmem_limit_bytes=24 * 2**20),
        cost_estimate=pl.CostEstimate(
            flops=10**9, bytes_accessed=10**7, transcendentals=10**6
        ),
        name="own_block",
    )(hidden, *shared)
    together = count - 1 if count <= 5 else 1
    return pl.pallas_call(
        functools.partial(join_kernel, count),
        out_shape=shape((BLOCK, EMBED), BF16),
        in_specs=[whole] * (count - 1 + 10 + 5),
        out_specs=whole,
        scratch_shapes=[
            pltpu.VMEM((max(count - 1, 1), BLOCK, EMBED), BF16),
            pltpu.VMEM((max(together, 1), 2, BLOCK, EMBED), BF16),
            pltpu.VMEM((2 * max(together, 1), TILES, PAD + BLOCK, 128), F32),
            pltpu.VMEM((count, 2, PAD, MIXED), F32),
            pltpu.VMEM((4, N, E), F32),
            pltpu.VMEM((PAD + EDGE, MIXED), F32),
            pltpu.VMEM((4, BLOCK, E), F32),
        ],
        compiler_params=pltpu.CompilerParams(vmem_limit_bytes=32 * 2**20),
        cost_estimate=pl.CostEstimate(
            flops=2 * 10**9, bytes_accessed=10**7, transcendentals=10**6
        ),
        name="join_blocks",
    )(
        *received,
        *shared,
        row(skip_gain),
        row(gate_gain),
        output_weight,
        *own,
    )


def solution(mesh):
    in_specs = (P(("batch", "seq"), None), P(), P(), P(), P(), P(), P(), P(), P(), P(), P())
    out_specs = P(("batch", "seq"), None)
    return jax.shard_map(
        on_device, mesh=mesh, in_specs=in_specs, out_specs=out_specs, check_vma=False
    )
```

```python
import functools

import jax
import jax.numpy as jnp
from jax import lax
from jax.experimental import pallas as pl
from jax.experimental.pallas import tpu as pltpu
from jax.sharding import PartitionSpec as P

EMBED = 512
E = 1024
N = 64
K = 4
BLOCK = 128
HEADS = 16
MIXED = E + 2 * N
TILES = MIXED // 128
PAIRS = E // 128
GROUPS = EMBED // 128
PAD = 8
EDGE = 16
eps = 1e-05
F32 = jnp.float32
BF16 = jnp.bfloat16


def dot(a, b):
    return jnp.dot(a, b, preferred_element_type=F32)


def dot_rows(a, b):
    return lax.dot_general(a, b, (((1,), (1,)), ((), ())), preferred_element_type=F32)


def iota(shape, axis):
    return lax.broadcasted_iota(jnp.int32, shape, axis)


def reversal():
    return (iota((128, 128), 0) + iota((128, 128), 1) == 127).astype(BF16)


def split(values, terms):
    parts = []
    for _ in range(terms):
        part = values.astype(BF16)
        parts.append(part)
        values = values - part.astype(F32)
    return parts


def exact_dot(values, mask):
    return sum(dot(part, mask) for part in split(values, 3))


def flip_lanes(rows, swap):
    return jnp.concatenate(
        [dot(rows[:, 128 * (GROUPS - 1 - g) : 128 * (GROUPS - g)], swap) for g in range(GROUPS)],
        axis=1,
    )


def both_normed(rows, gain, swap):
    floats = rows.astype(F32)
    scale = lax.rsqrt(jnp.mean(floats * floats, axis=-1, keepdims=True) + eps)
    flipped = flip_lanes(rows.astype(BF16), swap)
    return [(floats * scale * gain).astype(BF16), (flipped * scale * gain).astype(BF16)]


def half_silu(half):
    return half + half * jnp.tanh(half)


def column_of(row):
    shape = (HEADS, HEADS)
    return jnp.sum(
        jnp.where(iota(shape, 0) == iota(shape, 1), row, 0.0), axis=1, keepdims=True
    )


def log_decays(step_raw, step_bias, log_rate):
    v = step_raw + column_of(step_bias)
    u = jnp.exp(-jnp.abs(v))
    series = 1.0 / 7.0
    for order in range(6, 0, -1):
        series = 1.0 / order - u * series
    rest = jnp.where(u < 0.0625, u * series, jnp.log(1.0 + u))
    return -jnp.exp(column_of(log_rate)) * (jnp.maximum(v, 0.0) + rest)


def spread_heads(values, terms, start, stop, each):
    parts = jnp.concatenate(split(values, terms), axis=0)
    shape = (terms * HEADS, stop - start)
    head = (iota(shape, 1) + start) // each
    select = (iota(shape, 0) % HEADS == head).astype(BF16)
    return lax.dot_general(parts, select, (((0,), (0,)), ((), ())), preferred_element_type=F32)


def lanes_of(tile):
    return slice(tile * 128, tile * 128 + 128)


def chunks(width):
    return [(start, min(start + 256, width)) for start in range(0, width, 256)]


def filtered(source, at, lanes, taps, bias, backward=False, rows=BLOCK):
    result = bias[:, lanes]
    for k in range(K):
        low = at + ((K - 1) - k if backward else k - (K - 1))
        result = result + taps[k : k + 1, lanes] * source[low : low + rows]
    return result


def decay_kernel(*refs):
    sources, refs = refs[:5], refs[5:]
    (normal_ref, decay_ref, lift_ref), refs = refs[:3], refs[3:]
    held, semaphores = refs[:5], refs[5]
    copies = [
        pltpu.make_async_copy(sources[place], held[place], semaphores.at[place])
        for place in range(5)
    ]
    for copy in copies:
        copy.start()
    for copy in copies:
        copy.wait()
    x_ref, norm_gain_ref, step_weight_ref, step_bias_ref, log_rate_ref = held
    normal = jnp.concatenate(both_normed(x_ref[...], norm_gain_ref[...], reversal()), axis=0)
    normal_ref[...] = normal
    log_decay = log_decays(
        dot_rows(step_weight_ref[...], normal), step_bias_ref[...], log_rate_ref[...]
    )
    row, column = iota((BLOCK, BLOCK), 0), iota((BLOCK, BLOCK), 1)
    lower = row >= column
    both = jnp.concatenate([log_decay[:, :BLOCK], log_decay[:, BLOCK:]], axis=0)
    before = exact_dot(both, (row <= column).astype(BF16))
    after = exact_dot(both, (row >= column).astype(BF16))
    for flip in range(2):
        heads = slice(flip * HEADS, (flip + 1) * HEADS)
        for pair in range(PAIRS):
            low, high = 2 * pair * BLOCK, 2 * (pair + 1) * BLOCK
            from_start = spread_heads(before[heads], 3, low, high, BLOCK)
            to_end = spread_heads(after[heads], 3, low, high, BLOCK)
            for near in range(2):
                at = flip * HEADS + 2 * pair + near
                lanes = lanes_of(near)
                decay_ref[flip, 2 * pair + near] = jnp.exp(
                    jnp.where(
                        lower,
                        from_start[:, lanes] - before[at : at + 1],
                        to_end[:, lanes] - after[at : at + 1],
                    )
                )
        for start, stop in chunks(E):
            for way, rows in enumerate((before, after)):
                lift_ref[2 * flip + way, :, start:stop] = spread_heads(
                    jnp.exp(rows[heads]), 2, start, stop, N
                )


def own_kernel(
    normal_ref,
    input_weight_ref,
    conv_weight_ref,
    conv_bias_ref,
    activated_ref,
    edge_ref,
    silu_gate_ref,
    extended_ref,
):
    normal = normal_ref[...]
    taps, bias = 0.5 * conv_weight_ref[...], 0.5 * conv_bias_ref[...].reshape(1, MIXED)
    for start, stop in chunks(MIXED):
        mixed = dot(normal, input_weight_ref[:, E + start : E + stop]).astype(BF16).astype(F32)
        for flip in range(2):
            rows = mixed[flip * BLOCK : (flip + 1) * BLOCK]
            edge_ref[flip, :EDGE, start:stop] = rows[:EDGE]
            edge_ref[flip, EDGE:, start:stop] = rows[BLOCK - EDGE :]
            for tile in range(start // 128, stop // 128):
                lanes = lanes_of(tile)
                place = extended_ref.at[flip, tile]
                place[:PAD] = jnp.zeros((PAD, 128), F32)
                place[PAD + BLOCK :] = jnp.zeros((PAD, 128), F32)
                place[PAD : PAD + BLOCK] = rows[:, tile * 128 - start : tile * 128 - start + 128]
                for way in range(2):
                    half = filtered(place, PAD, lanes, taps, bias, way == 1)
                    activated_ref[2 * flip + way, :, lanes] = half_silu(half).astype(BF16)
    for start, stop in chunks(E):
        gate = dot(normal, input_weight_ref[:, start:stop]).astype(BF16).astype(F32)
        gate = half_silu(0.5 * gate)
        for flip in range(2):
            silu_gate_ref[flip, :, start:stop] = gate[flip * BLOCK : (flip + 1) * BLOCK]


def chain_rows(mask, index, block, gain, swap):
    row, column = iota((BLOCK, BLOCK), 0), iota((BLOCK, BLOCK), 1)
    order = jnp.where((index ^ mask) < index, row, 127 - row) == column
    return both_normed(dot(order.astype(BF16), block), gain, swap)


def ahead_kernel(
    mask,
    block_ref,
    norm_gain_ref,
    input_weight_ref,
    step_weight_ref,
    conv_weight_ref,
    conv_bias_ref,
    step_bias_ref,
    log_rate_ref,
    activated_ref,
    edge_ref,
    log_decay_ref,
    extended_ref,
):
    index = lax.axis_index("seq")
    normal = jnp.concatenate(
        chain_rows(mask, index, block_ref[...], norm_gain_ref[...], reversal()), axis=0
    )
    log_decay_ref[...] = log_decays(
        dot_rows(step_weight_ref[...], normal), step_bias_ref[...], log_rate_ref[...]
    )
    taps, bias = 0.5 * conv_weight_ref[...], 0.5 * conv_bias_ref[...].reshape(1, MIXED)
    for start, stop in chunks(MIXED):
        mixed = dot(normal, input_weight_ref[:, E + start : E + stop]).astype(BF16).astype(F32)
        for flip in range(2):
            rows = mixed[flip * BLOCK : (flip + 1) * BLOCK]
            edge_ref[flip, :EDGE, start:stop] = rows[:EDGE]
            edge_ref[flip, EDGE:, start:stop] = rows[BLOCK - PAD :]
            for tile in range(start // 128, stop // 128):
                lanes = lanes_of(tile)
                place = extended_ref.at[flip, tile]
                place[:PAD] = jnp.zeros((PAD, 128), F32)
                place[PAD:] = rows[:, tile * 128 - start : tile * 128 - start + 128]
                half = filtered(place, PAD, lanes, taps, bias)
                activated_ref[flip, :, lanes] = half_silu(half).astype(BF16)


def join_kernel(count, top, *refs):
    others = [mask for mask in range(1, count) if mask != top]
    received, refs = refs[: len(others)], refs[len(others) :]
    (
        norm_gain_ref,
        input_weight_ref,
        step_weight_ref,
        conv_weight_ref,
        conv_bias_ref,
        step_bias_ref,
        log_rate_ref,
        skip_gain_ref,
        gate_gain_ref,
        output_weight_ref,
        decay_ref,
        lift_ref,
        activated_ref,
        edge_ref,
        silu_gate_ref,
        ahead_ref,
        ahead_edge_ref,
        ahead_log_decay_ref,
        out_ref,
        normal_ref,
        extended_ref,
        halo_ref,
        memory_ref,
        window_ref,
        patch_ref,
        gated_ref,
    ) = refs
    index = lax.axis_index("seq")
    swap = reversal()
    row, column = iota((BLOCK, BLOCK), 0), iota((BLOCK, BLOCK), 1)
    lower, upper = row >= column, row <= column
    left = column < N
    taps, bias = 0.5 * conv_weight_ref[...], 0.5 * conv_bias_ref[...].reshape(1, MIXED)

    def halo_of(block, flip):
        exists = jnp.where((block >= 0) & (block < count), 1.0, 0.0)
        place = jnp.clip((block ^ index) - 1, 0, count - 2)
        return exists * halo_ref[place, flip]

    for place, mask in enumerate(others):
        block = received[place][...]
        for flip, part in enumerate(chain_rows(mask, index, block, norm_gain_ref[...], swap)):
            low = (2 * place + flip) * BLOCK
            normal_ref[low : low + BLOCK] = part
    normal = normal_ref[...]
    log_decay = log_decays(
        dot_rows(step_weight_ref[...], normal), step_bias_ref[...], log_rate_ref[...]
    )
    pieces = {}
    for flip in range(2):
        for place, mask in enumerate(others):
            low = (2 * place + flip) * BLOCK
            pieces[mask, flip] = log_decay[:, low : low + BLOCK]
        pieces[top, flip] = ahead_log_decay_ref[:, flip * BLOCK : (flip + 1) * BLOCK]
    parts = [(mask, flip) for mask in range(1, count) for flip in range(2)]
    tails = exact_dot(
        jnp.concatenate([pieces[part] for part in parts], axis=0), (row > column).astype(BF16)
    )
    wholes = {part: jnp.sum(pieces[part], axis=1, keepdims=True) for part in parts}
    faded = [[], []]
    for at, (mask, flip) in enumerate(parts):
        tail = tails[at * HEADS : (at + 1) * HEADS]
        block = index ^ mask
        for other in range(1, count):
            if other != mask:
                between = index ^ other
                later = ((block < between) & (between < index)) | (
                    (index < between) & (between < block)
                )
                tail = tail + jnp.where(later, wholes[other, flip], 0.0)
        faded[flip].append(jnp.exp(tail))
    faded = [jnp.concatenate(rows, axis=1) for rows in faded]

    for flip in range(2):
        halo_ref[top - 1, flip] = ahead_edge_ref[flip, EDGE:]
    writers = [None, None]
    order = chunks(MIXED)
    for start, stop in order[-1:] + order[:-1]:
        mixed = dot(normal, input_weight_ref[:, E + start : E + stop]).astype(BF16).astype(F32)
        for place, mask in enumerate(others):
            for flip in range(2):
                low = (2 * place + flip) * BLOCK
                halo_ref[mask - 1, flip, :, start:stop] = mixed[low + BLOCK - PAD : low + BLOCK]
        for flip in range(2):
            acted = {}
            for mask in range(1, count):
                block = index ^ mask
                before = jnp.where(block < index, block - 1, block + 1)
                halo = halo_of(before, flip)[:, start:stop]
                if mask == top:
                    near = []
                    for tile in range(start // 128, stop // 128):
                        lanes = lanes_of(tile)
                        spot = patch_ref.at[flip, tile]
                        spot[:PAD] = halo[:, tile * 128 - start : tile * 128 - start + 128]
                        spot[PAD:] = ahead_edge_ref[flip, :EDGE, lanes]
                        half = filtered(spot, PAD, lanes, taps, bias, False, EDGE)
                        patch = half_silu(half).astype(BF16)
                        near.append(
                            jnp.concatenate([patch, ahead_ref[flip, EDGE:, lanes]], axis=0)
                        )
                    acted[mask] = jnp.concatenate(near, axis=1)
                    continue
                place = others.index(mask)
                low = (2 * place + flip) * BLOCK
                near = []
                for tile in range(start // 128, stop // 128):
                    at = tile * 128 - start
                    spot = extended_ref.at[2 * place + flip, tile]
                    spot[:PAD] = halo[:, at : at + 128]
                    spot[PAD:] = mixed[low : low + BLOCK, at : at + 128]
                    half = filtered(spot, PAD, lanes_of(tile), taps, bias)
                    near.append(half_silu(half).astype(BF16))
                acted[mask] = jnp.concatenate(near, axis=1)
            if start == E:
                sides = []
                for mask in range(1, count):
                    maps = acted[mask].T[:N]
                    earlier = jnp.where((index ^ mask) < index, 1.0, 0.0).astype(BF16)
                    later = jnp.where((index ^ mask) < index, 0.0, 1.0).astype(BF16)
                    sides.append(jnp.concatenate([maps * earlier, maps * later], axis=0))
                writers[flip] = jnp.concatenate(sides, axis=1)
                continue
            fade = spread_heads(faded[flip], 2, start, stop, N)
            decayed = [
                (fade[at * BLOCK : (at + 1) * BLOCK] * acted[at + 1].astype(F32)).astype(BF16)
                for at in range(count - 1)
            ]
            memory = dot(writers[flip], jnp.concatenate(decayed, axis=0))
            for way in range(2):
                high, low = split(memory[way * N : (way + 1) * N], 2)
                memory_ref[2 * flip + way, :N, start:stop] = high
                memory_ref[2 * flip + way, N:, start:stop] = low

    skip = wide_row(skip_gain_ref[...])
    for flip in range(2):
        for way in range(2):
            chain = 2 * flip + way
            spot = window_ref.at[chain]
            if way == 0:
                spot[:PAD] = halo_of(index - 1, flip)
                spot[PAD:] = edge_ref[flip, :EDGE]
            else:
                halo = halo_of(index + 1, flip)
                spot[:EDGE] = edge_ref[flip, EDGE:]
                for step in range(K - 1):
                    spot[EDGE + step : EDGE + step + 1] = halo[PAD - 1 - step : PAD - step]
            at = PAD if way == 0 else 0
            half = filtered(spot, at, slice(0, MIXED), taps, bias, way == 1, EDGE)
            patch = half_silu(half).astype(BF16)

            def acted(tile):
                lanes = lanes_of(tile)
                if way == 0:
                    near = [patch[:, lanes], activated_ref[chain, EDGE:, lanes]]
                else:
                    near = [activated_ref[chain, : BLOCK - EDGE, lanes], patch[:, lanes]]
                return jnp.concatenate(near, axis=0)

            maps = acted(PAIRS)
            writer, reader = maps[:, :N], maps[:, N:]
            scores = jnp.where(lower if way == 0 else upper, dot_rows(reader, writer), 0.0)
            squares = jnp.zeros((BLOCK, 128), F32)
            doubled = jnp.concatenate([reader, reader], axis=1)
            for pair in range(PAIRS):
                lanes = lanes_of(pair)
                signal = acted(pair)
                zeros = jnp.zeros_like(signal)
                signals = jnp.concatenate(
                    [jnp.where(left, signal, zeros), jnp.where(left, zeros, signal)], axis=0
                )
                weights = jnp.concatenate(
                    [
                        (decay_ref[flip, 2 * pair + near] * scores).astype(BF16)
                        for near in range(2)
                    ],
                    axis=1,
                )
                inside = dot(weights, signals)
                carried = dot(doubled, memory_ref[chain, :, lanes])
                inside = inside + lift_ref[chain, :, lanes] * carried
                gated = inside + skip[:, lanes] * signal.astype(F32)
                gated = gated * silu_gate_ref[flip, :, lanes]
                squares = squares + gated * gated
                gated_ref[chain, :, lanes] = gated
            scale = lax.rsqrt(jnp.sum(squares, axis=1, keepdims=True) * (1.0 / E) + eps)
            for pair in range(PAIRS):
                lanes = lanes_of(pair)
                gated_ref[chain, :, lanes] = (
                    gated_ref[chain, :, lanes] * scale * gate_gain_ref[:, lanes]
                )

    normed = gated_ref[...].astype(BF16).reshape(4 * BLOCK, E)
    made = dot(normed, output_weight_ref[...])
    straight, crossed = made[: 2 * BLOCK], made[2 * BLOCK :]
    high, low = split(crossed, 2)
    both = straight + flip_lanes(high, swap) + flip_lanes(low, swap)
    backward = both[BLOCK:].astype(BF16).astype(F32)
    out_ref[...] = (both[:BLOCK] + backward).astype(BF16)


def wide_row(row):
    select = (iota((HEADS, E), 1) // N == iota((HEADS, E), 0)).astype(BF16)
    return exact_dot(jnp.broadcast_to(row, (8, HEADS)), select)[:1]


def swapped(rows, step, count):
    return lax.ppermute(rows, "seq", [(i, i ^ step) for i in range(count)])


def on_device(
    hidden,
    norm_gain,
    input_weight,
    step_weight,
    conv_weight,
    conv_bias,
    step_bias,
    log_rate,
    skip_gain,
    gate_gain,
    output_weight,
):
    count = lax.axis_size("seq")
    top = count // 2
    row = lambda vector: vector.reshape(1, -1)
    whole = pl.BlockSpec(memory_space=pltpu.VMEM)
    shape = jax.ShapeDtypeStruct
    gain, step_map = row(norm_gain), step_weight.T
    step_bias, log_rate = row(step_bias), row(log_rate)
    across = swapped(hidden, top, count)

    def call(kernel, name, outs, scratch, operands, flops, limit, spec=whole):
        return pl.pallas_call(
            kernel,
            out_shape=outs,
            in_specs=[spec] * len(operands),
            out_specs=[whole] * len(outs),
            scratch_shapes=scratch,
            compiler_params=pltpu.CompilerParams(vmem_limit_bytes=limit * 2**20),
            cost_estimate=pl.CostEstimate(
                flops=flops, bytes_accessed=10**7, transcendentals=10**6
            ),
            name=name,
        )(*operands)

    small = (hidden, gain, step_map, step_bias, log_rate)
    normal, decay, lift = call(
        decay_kernel,
        "decays",
        [
            shape((2 * BLOCK, EMBED), BF16),
            shape((2, HEADS, BLOCK, BLOCK), F32),
            shape((4, BLOCK, E), F32),
        ],
        [
            *[pltpu.VMEM(part.shape, part.dtype) for part in small],
            pltpu.SemaphoreType.DMA((5,)),
        ],
        [pltpu.with_memory_space_constraint(part, pltpu.HBM) for part in small],
        10**9,
        12,
        pl.BlockSpec(memory_space=pltpu.HBM),
    )
    own = call(
        own_kernel,
        "own_rows",
        [
            shape((4, BLOCK, MIXED), BF16),
            shape((2, 2 * EDGE, MIXED), F32),
            shape((2, BLOCK, E), F32),
        ],
        [pltpu.VMEM((2, TILES, BLOCK + 2 * PAD, 128), F32)],
        [normal, input_weight, conv_weight, conv_bias],
        10**9,
        12,
    )
    start, across, decay, lift, *own = lax.optimization_barrier(
        (hidden, across, decay, lift, *own)
    )
    received = {0: start, top: across}
    for bit in reversed(range(top.bit_length() - 1)):
        for mask in sorted(received):
            received[mask | 1 << bit] = swapped(received[mask], 1 << bit, count)
    shared = [gain, input_weight, step_map, conv_weight, conv_bias, step_bias, log_rate]
    ahead = call(
        functools.partial(ahead_kernel, top),
        "across_rows",
        [
            shape((2, BLOCK, MIXED), BF16),
            shape((2, EDGE + PAD, MIXED), F32),
            shape((HEADS, 2 * BLOCK), F32),
        ],
        [pltpu.VMEM((2, TILES, PAD + BLOCK, 128), F32)],
        [across, *shared],
        10**9,
        12,
    )
    others = [mask for mask in range(1, count) if mask != top]
    (out,) = call(
        functools.partial(join_kernel, count, top),
        "join_blocks",
        [shape((BLOCK, EMBED), BF16)],
        [
            pltpu.VMEM((2 * len(others) * BLOCK, EMBED), BF16),
            pltpu.VMEM((2 * len(others), TILES, PAD + BLOCK, 128), F32),
            pltpu.VMEM((count - 1, 2, PAD, MIXED), F32),
            pltpu.VMEM((4, 2 * N, E), BF16),
            pltpu.VMEM((4, PAD + EDGE, MIXED), F32),
            pltpu.VMEM((2, TILES, PAD + EDGE, 128), F32),
            pltpu.VMEM((4, BLOCK, E), F32),
        ],
        [
            *[received[mask] for mask in others],
            *shared,
            row(skip_gain),
            row(gate_gain),
            output_weight,
            decay,
            lift,
            *own,
            *ahead,
        ],
        2 * 10**9,
        18 + 2 * len(others),
    )
    return out


def solution(mesh):
    in_specs = (P(("batch", "seq"), None), P(), P(), P(), P(), P(), P(), P(), P(), P(), P())
    out_specs = P(("batch", "seq"), None)
    return jax.shard_map(
        on_device, mesh=mesh, in_specs=in_specs, out_specs=out_specs, check_vma=False
    )
```

```python
import functools

import jax
import jax.numpy as jnp
from jax import lax
from jax.experimental import pallas as pl
from jax.experimental.pallas import tpu as pltpu
from jax.sharding import PartitionSpec as P

EMBED = 512
E = 1024
N = 64
K = 4
BLOCK = 128
HEADS = 16
MIXED = E + 2 * N
TILES = MIXED // 128
PAIRS = E // 128
GROUPS = EMBED // 128
PAD = 8
EDGE = 16
eps = 1e-05
F32 = jnp.float32
BF16 = jnp.bfloat16


def dot(a, b):
    return jnp.dot(a, b, preferred_element_type=F32)


def dot_rows(a, b):
    return lax.dot_general(a, b, (((1,), (1,)), ((), ())), preferred_element_type=F32)


def iota(shape, axis):
    return lax.broadcasted_iota(jnp.int32, shape, axis)


def reversal():
    return (iota((128, 128), 0) + iota((128, 128), 1) == 127).astype(BF16)


def split(values, terms):
    parts = []
    for _ in range(terms):
        part = values.astype(BF16)
        parts.append(part)
        values = values - part.astype(F32)
    return parts


def exact_dot(values, mask):
    return sum(dot(part, mask) for part in split(values, 3))


def flip_lanes(rows, swap):
    return jnp.concatenate(
        [dot(rows[:, 128 * (GROUPS - 1 - g) : 128 * (GROUPS - g)], swap) for g in range(GROUPS)],
        axis=1,
    )


def both_normed(rows, gain, swap):
    floats = rows.astype(F32)
    scale = lax.rsqrt(jnp.mean(floats * floats, axis=-1, keepdims=True) + eps)
    flipped = flip_lanes(rows.astype(BF16), swap)
    return [(floats * scale * gain).astype(BF16), (flipped * scale * gain).astype(BF16)]


def half_silu(half):
    return half + half * jnp.tanh(half)


def column_of(row):
    shape = (HEADS, HEADS)
    return jnp.sum(
        jnp.where(iota(shape, 0) == iota(shape, 1), row, 0.0), axis=1, keepdims=True
    )


def log_decays(step_raw, step_bias, log_rate):
    v = step_raw + column_of(step_bias)
    u = jnp.exp(-jnp.abs(v))
    series = 1.0 / 7.0
    for order in range(6, 0, -1):
        series = 1.0 / order - u * series
    rest = jnp.where(u < 0.0625, u * series, jnp.log(1.0 + u))
    return -jnp.exp(column_of(log_rate)) * (jnp.maximum(v, 0.0) + rest)


def selectors(terms, heads):
    shape = (terms * HEADS, 256)
    head = iota(shape, 0) & (HEADS - 1)
    near = iota(shape, 1) >> (8 - (heads.bit_length() - 1))
    return [(head - near == low).astype(BF16) for low in range(0, HEADS, heads)]


def stacked_split(values, terms):
    return jnp.concatenate(split(values, terms), axis=0)


def dot_columns(a, b):
    return lax.dot_general(a, b, (((0,), (0,)), ((), ())), preferred_element_type=F32)


def lanes_of(tile):
    return slice(tile * 128, tile * 128 + 128)


def chunks(width):
    return [(start, min(start + 256, width)) for start in range(0, width, 256)]


def filtered(source, at, lanes, taps, bias, backward=False, rows=BLOCK):
    result = bias[:, lanes]
    for k in range(K):
        low = at + ((K - 1) - k if backward else k - (K - 1))
        result = result + taps[k : k + 1, lanes] * source[low : low + rows]
    return result


def decay_kernel(*refs):
    sources, refs = refs[:5], refs[5:]
    (normal_ref, decay_ref, lift_ref), refs = refs[:3], refs[3:]
    held, semaphores = refs[:5], refs[5]
    copies = [
        pltpu.make_async_copy(sources[place], held[place], semaphores.at[place])
        for place in range(5)
    ]
    for copy in copies:
        copy.start()
    for copy in copies:
        copy.wait()
    x_ref, norm_gain_ref, step_weight_ref, step_bias_ref, log_rate_ref = held
    normal = jnp.concatenate(both_normed(x_ref[...], norm_gain_ref[...], reversal()), axis=0)
    normal_ref[...] = normal
    log_decay = log_decays(
        dot_rows(step_weight_ref[...], normal), step_bias_ref[...], log_rate_ref[...]
    )
    row, column = iota((BLOCK, BLOCK), 0), iota((BLOCK, BLOCK), 1)
    lower = row >= column
    both = jnp.concatenate([log_decay[:, :BLOCK], log_decay[:, BLOCK:]], axis=0)
    before = exact_dot(both, (row <= column).astype(BF16))
    after = exact_dot(both, (row >= column).astype(BF16))
    twos, fours = selectors(3, 2), selectors(1, 4)
    for flip in range(2):
        heads = slice(flip * HEADS, (flip + 1) * HEADS)
        ones = jnp.ones((3 * HEADS, BLOCK), BF16)
        sides = []
        for rows in (before, after):
            parts = stacked_split(rows[heads], 3)
            sides.append((jnp.concatenate([parts, ones], axis=0), jnp.concatenate([-parts] * 2, 1)))

        def spread(side, pair):
            plus, minus = sides[side]
            return dot_columns(plus, jnp.concatenate([twos[pair], twos[pair] * minus], axis=0))

        for pair in range(PAIRS):
            from_start, to_end = spread(0, pair), spread(1, pair)
            for near in range(2):
                lanes = lanes_of(near)
                decay_ref[flip, 2 * pair + near] = jnp.exp(
                    jnp.where(lower, from_start[:, lanes], to_end[:, lanes])
                ).astype(BF16)
        for way, rows in enumerate((before, after)):
            lifts = jnp.exp(rows[heads]).astype(BF16)
            for place, (start, stop) in enumerate(chunks(E)):
                lift_ref[2 * flip + way, :, start:stop] = dot_columns(lifts, fours[place]).astype(
                    BF16
                )


def own_kernel(
    normal_ref,
    input_weight_ref,
    conv_weight_ref,
    conv_bias_ref,
    activated_ref,
    edge_ref,
    silu_gate_ref,
    extended_ref,
):
    normal = normal_ref[...]
    taps, bias = 0.5 * conv_weight_ref[...], 0.5 * conv_bias_ref[...].reshape(1, MIXED)
    for start, stop in chunks(MIXED):
        mixed = dot(normal, input_weight_ref[:, E + start : E + stop])
        for flip in range(2):
            rows = mixed[flip * BLOCK : (flip + 1) * BLOCK]
            edge_ref[flip, :EDGE, start:stop] = rows[:EDGE]
            edge_ref[flip, EDGE:, start:stop] = rows[BLOCK - EDGE :]
            for tile in range(start // 128, stop // 128):
                lanes = lanes_of(tile)
                place = extended_ref.at[flip, tile]
                place[:PAD] = jnp.zeros((PAD, 128), F32)
                place[PAD + BLOCK :] = jnp.zeros((PAD, 128), F32)
                place[PAD : PAD + BLOCK] = rows[:, tile * 128 - start : tile * 128 - start + 128]
                for way in range(2):
                    half = filtered(place, PAD, lanes, taps, bias, way == 1)
                    activated_ref[2 * flip + way, :, lanes] = half_silu(half).astype(BF16)
    for start, stop in chunks(E):
        gate = dot(normal, input_weight_ref[:, start:stop])
        gate = half_silu(0.5 * gate)
        for flip in range(2):
            silu_gate_ref[flip, :, start:stop] = gate[flip * BLOCK : (flip + 1) * BLOCK]


def chain_rows(mask, index, block, gain, swap):
    row, column = iota((BLOCK, BLOCK), 0), iota((BLOCK, BLOCK), 1)
    order = jnp.where((index ^ mask) < index, row, 127 - row) == column
    return both_normed(dot(order.astype(BF16), block), gain, swap)


def ahead_kernel(
    mask,
    block_ref,
    norm_gain_ref,
    input_weight_ref,
    step_weight_ref,
    conv_weight_ref,
    conv_bias_ref,
    step_bias_ref,
    log_rate_ref,
    activated_ref,
    edge_ref,
    log_decay_ref,
    extended_ref,
):
    index = lax.axis_index("seq")
    normal = jnp.concatenate(
        chain_rows(mask, index, block_ref[...], norm_gain_ref[...], reversal()), axis=0
    )
    log_decay_ref[...] = log_decays(
        dot_rows(step_weight_ref[...], normal), step_bias_ref[...], log_rate_ref[...]
    )
    taps, bias = 0.5 * conv_weight_ref[...], 0.5 * conv_bias_ref[...].reshape(1, MIXED)
    for start, stop in chunks(MIXED):
        mixed = dot(normal, input_weight_ref[:, E + start : E + stop])
        for flip in range(2):
            rows = mixed[flip * BLOCK : (flip + 1) * BLOCK]
            edge_ref[flip, :EDGE, start:stop] = rows[:EDGE]
            edge_ref[flip, EDGE:, start:stop] = rows[BLOCK - PAD :]
            for tile in range(start // 128, stop // 128):
                lanes = lanes_of(tile)
                place = extended_ref.at[flip, tile]
                place[:PAD] = jnp.zeros((PAD, 128), F32)
                place[PAD:] = rows[:, tile * 128 - start : tile * 128 - start + 128]
                half = filtered(place, PAD, lanes, taps, bias)
                activated_ref[flip, :, lanes] = half_silu(half).astype(BF16)


def join_kernel(count, top, *refs):
    others = [mask for mask in range(1, count) if mask != top]
    received, refs = refs[: len(others)], refs[len(others) :]
    (
        norm_gain_ref,
        input_weight_ref,
        step_weight_ref,
        conv_weight_ref,
        conv_bias_ref,
        step_bias_ref,
        log_rate_ref,
        skip_gain_ref,
        gate_gain_ref,
        output_weight_ref,
        decay_ref,
        lift_ref,
        activated_ref,
        edge_ref,
        silu_gate_ref,
        ahead_ref,
        ahead_edge_ref,
        ahead_log_decay_ref,
        out_ref,
        normal_ref,
        extended_ref,
        memory_ref,
        window_ref,
        patch_ref,
        gated_ref,
    ) = refs
    index = lax.axis_index("seq")
    swap = reversal()
    row, column = iota((BLOCK, BLOCK), 0), iota((BLOCK, BLOCK), 1)
    lower, upper = row >= column, row <= column
    left, right = (column < N).astype(BF16), (column >= N).astype(BF16)
    taps, bias = 0.5 * conv_weight_ref[...], 0.5 * conv_bias_ref[...].reshape(1, MIXED)

    def picked(rows, block):
        result = jnp.zeros((PAD, rows[top].shape[1]), F32)
        for mask, part in rows.items():
            result = jnp.where((index ^ mask) == block, part, result)
        return result

    for place, mask in enumerate(others):
        block = received[place][...]
        for flip, part in enumerate(chain_rows(mask, index, block, norm_gain_ref[...], swap)):
            low = (2 * place + flip) * BLOCK
            normal_ref[low : low + BLOCK] = part
    normal = normal_ref[...]
    log_decay = log_decays(
        dot_rows(step_weight_ref[...], normal), step_bias_ref[...], log_rate_ref[...]
    )
    pieces = {}
    for flip in range(2):
        for place, mask in enumerate(others):
            low = (2 * place + flip) * BLOCK
            pieces[mask, flip] = log_decay[:, low : low + BLOCK]
        pieces[top, flip] = ahead_log_decay_ref[:, flip * BLOCK : (flip + 1) * BLOCK]
    parts = [(mask, flip) for mask in range(1, count) for flip in range(2)]
    tails = exact_dot(
        jnp.concatenate([pieces[part] for part in parts], axis=0), (row > column).astype(BF16)
    )
    wholes = {part: jnp.sum(pieces[part], axis=1, keepdims=True) for part in parts}
    faded = [[], []]
    for at, (mask, flip) in enumerate(parts):
        tail = tails[at * HEADS : (at + 1) * HEADS]
        block = index ^ mask
        for other in range(1, count):
            if other != mask:
                between = index ^ other
                later = ((block < between) & (between < index)) | (
                    (index < between) & (between < block)
                )
                tail = tail + jnp.where(later, wholes[other, flip], 0.0)
        faded[flip].append(jnp.exp(tail))
    faded = [jnp.concatenate(rows, axis=1).astype(BF16) for rows in faded]
    fours = selectors(1, 4)

    writers = [None, None]
    order = chunks(MIXED)
    order = order[-1:] + order[:-1]

    def project(place):
        start, stop = order[place]
        return dot(normal, input_weight_ref[:, E + start : E + stop])

    def fade_of(place, flip):
        return dot_columns(faded[flip], fours[order[place][0] // 256]).astype(BF16)

    ready, coming = project(0), None
    for turn, (start, stop) in enumerate(order):
        mixed = ready
        if turn + 1 < len(order):
            ready = project(turn + 1)
            fades, coming = coming, [fade_of(turn + 1, flip) for flip in range(2)]
        else:
            fades = coming
        for flip in range(2):
            acted, last = {}, {top: ahead_edge_ref[flip, EDGE:, start:stop]}
            for place, mask in enumerate(others):
                low = (2 * place + flip) * BLOCK
                last[mask] = mixed[low + BLOCK - PAD : low + BLOCK]
            window_ref[2 * flip, :PAD, start:stop] = picked(last, index - 1)
            behind = picked(last, index + 1)
            for step in range(K - 1):
                spot = slice(EDGE + step, EDGE + step + 1)
                window_ref[2 * flip + 1, spot, start:stop] = behind[PAD - 1 - step : PAD - step]
            for mask in range(1, count):
                block = index ^ mask
                halo = picked(last, jnp.where(block < index, block - 1, block + 1))
                if mask == top:
                    near = []
                    for tile in range(start // 128, stop // 128):
                        lanes = lanes_of(tile)
                        spot = patch_ref.at[flip, tile]
                        spot[:PAD] = halo[:, tile * 128 - start : tile * 128 - start + 128]
                        spot[PAD:] = ahead_edge_ref[flip, :EDGE, lanes]
                        half = filtered(spot, PAD, lanes, taps, bias, False, EDGE)
                        patch = half_silu(half).astype(BF16)
                        near.append(
                            jnp.concatenate([patch, ahead_ref[flip, EDGE:, lanes]], axis=0)
                        )
                    acted[mask] = jnp.concatenate(near, axis=1)
                    continue
                place = others.index(mask)
                low = (2 * place + flip) * BLOCK
                near = []
                for tile in range(start // 128, stop // 128):
                    at = tile * 128 - start
                    spot = extended_ref.at[2 * place + flip, tile]
                    spot[:PAD] = halo[:, at : at + 128]
                    spot[PAD:] = mixed[low : low + BLOCK, at : at + 128]
                    half = filtered(spot, PAD, lanes_of(tile), taps, bias)
                    near.append(half_silu(half).astype(BF16))
                acted[mask] = jnp.concatenate(near, axis=1)
            if start == E:
                sides = []
                for mask in range(1, count):
                    maps = acted[mask].T[:N]
                    earlier = jnp.where((index ^ mask) < index, 1.0, 0.0).astype(BF16)
                    later = jnp.where((index ^ mask) < index, 0.0, 1.0).astype(BF16)
                    sides.append(jnp.concatenate([maps * earlier, maps * later], axis=0))
                writers[flip] = jnp.concatenate(sides, axis=1)
                continue
            fade = fades[flip]
            decayed = [
                fade[at * BLOCK : (at + 1) * BLOCK] * acted[at + 1]
                for at in range(count - 1)
            ]
            memory = dot(writers[flip], jnp.concatenate(decayed, axis=0))
            for way in range(2):
                kept = memory[way * N : (way + 1) * N]
                even = (iota(kept.shape, 1) & N) == 0
                chain = 2 * flip + way
                memory_ref[chain, :N, start:stop] = jnp.where(even, kept, 0.0).astype(BF16)
                memory_ref[chain, N:, start:stop] = jnp.where(even, 0.0, kept).astype(BF16)

    skip = wide_row(skip_gain_ref[...])
    for flip in range(2):
        for way in range(2):
            chain = 2 * flip + way
            spot = window_ref.at[chain]
            if way == 0:
                spot[PAD:] = edge_ref[flip, :EDGE]
            else:
                spot[:EDGE] = edge_ref[flip, EDGE:]
            at = PAD if way == 0 else 0
            half = filtered(spot, at, slice(0, MIXED), taps, bias, way == 1, EDGE)
            patch = half_silu(half).astype(BF16)

            def acted(tile):
                lanes = lanes_of(tile)
                if way == 0:
                    near = [patch[:, lanes], activated_ref[chain, EDGE:, lanes]]
                else:
                    near = [activated_ref[chain, : BLOCK - EDGE, lanes], patch[:, lanes]]
                return jnp.concatenate(near, axis=0)

            maps = acted(PAIRS)
            writer, reader = maps[:, :N], maps[:, N:]
            scores = jnp.where(lower if way == 0 else upper, dot_rows(reader, writer), 0.0)
            scores = scores.astype(BF16)
            squares = jnp.zeros((BLOCK, 128), F32)
            doubled = jnp.concatenate([reader, reader], axis=1)
            for pair in range(PAIRS):
                lanes = lanes_of(pair)
                signal = acted(pair)
                signals = jnp.concatenate(
                    [signal * left, signal * right, memory_ref[chain, :, lanes]], axis=0
                )
                weights = jnp.concatenate(
                    [
                        decay_ref[flip, 2 * pair + near] * scores
                        for near in range(2)
                    ]
                    + [lift_ref[chain, :, lanes] * doubled],
                    axis=1,
                )
                inside = dot(weights, signals)
                gated = inside + skip[:, lanes] * signal.astype(F32)
                gated = gated * silu_gate_ref[flip, :, lanes]
                squares = squares + gated * gated
                gated_ref[chain, :, lanes] = gated
            scale = lax.rsqrt(jnp.sum(squares, axis=1, keepdims=True) * (1.0 / E) + eps)
            for pair in range(PAIRS):
                lanes = lanes_of(pair)
                gated_ref[chain, :, lanes] = (
                    gated_ref[chain, :, lanes] * scale * gate_gain_ref[:, lanes]
                )

    normed = gated_ref[...].astype(BF16).reshape(4 * BLOCK, E)
    made = dot(normed, output_weight_ref[...])
    straight, crossed = made[: 2 * BLOCK], made[2 * BLOCK :]
    high, low = split(crossed, 2)
    both = straight + flip_lanes(high, swap) + flip_lanes(low, swap)
    backward = both[BLOCK:].astype(BF16).astype(F32)
    out_ref[...] = (both[:BLOCK] + backward).astype(BF16)


def wide_row(row):
    select = (iota((HEADS, E), 1) // N == iota((HEADS, E), 0)).astype(BF16)
    return exact_dot(jnp.broadcast_to(row, (8, HEADS)), select)[:1]


def swapped(rows, step, count):
    return lax.ppermute(rows, "seq", [(i, i ^ step) for i in range(count)])


def on_device(
    hidden,
    norm_gain,
    input_weight,
    step_weight,
    conv_weight,
    conv_bias,
    step_bias,
    log_rate,
    skip_gain,
    gate_gain,
    output_weight,
):
    count = lax.axis_size("seq")
    top = count // 2
    row = lambda vector: vector.reshape(1, -1)
    whole = pl.BlockSpec(memory_space=pltpu.VMEM)
    shape = jax.ShapeDtypeStruct
    gain, step_map = row(norm_gain), step_weight.T
    step_bias, log_rate = row(step_bias), row(log_rate)
    across = swapped(hidden, top, count)

    def call(kernel, name, outs, scratch, operands, flops, limit, spec=whole):
        return pl.pallas_call(
            kernel,
            out_shape=outs,
            in_specs=[spec] * len(operands),
            out_specs=[whole] * len(outs),
            scratch_shapes=scratch,
            compiler_params=pltpu.CompilerParams(vmem_limit_bytes=limit * 2**20),
            cost_estimate=pl.CostEstimate(
                flops=flops, bytes_accessed=10**7, transcendentals=10**6
            ),
            name=name,
        )(*operands)

    small = (hidden, gain, step_map, step_bias, log_rate)
    normal, decay, lift = call(
        decay_kernel,
        "decays",
        [
            shape((2 * BLOCK, EMBED), BF16),
            shape((2, HEADS, BLOCK, BLOCK), BF16),
            shape((4, BLOCK, E), BF16),
        ],
        [
            *[pltpu.VMEM(part.shape, part.dtype) for part in small],
            pltpu.SemaphoreType.DMA((5,)),
        ],
        [pltpu.with_memory_space_constraint(part, pltpu.HBM) for part in small],
        10**9,
        12,
        pl.BlockSpec(memory_space=pltpu.HBM),
    )
    own = call(
        own_kernel,
        "own_rows",
        [
            shape((4, BLOCK, MIXED), BF16),
            shape((2, 2 * EDGE, MIXED), F32),
            shape((2, BLOCK, E), F32),
        ],
        [pltpu.VMEM((2, TILES, BLOCK + 2 * PAD, 128), F32)],
        [normal, input_weight, conv_weight, conv_bias],
        10**9,
        12,
    )
    start, across, decay, lift, *own = lax.optimization_barrier(
        (hidden, across, decay, lift, *own)
    )
    received = {0: start, top: across}
    for bit in reversed(range(top.bit_length() - 1)):
        for mask in sorted(received):
            received[mask | 1 << bit] = swapped(received[mask], 1 << bit, count)
    shared = [gain, input_weight, step_map, conv_weight, conv_bias, step_bias, log_rate]
    ahead = call(
        functools.partial(ahead_kernel, top),
        "across_rows",
        [
            shape((2, BLOCK, MIXED), BF16),
            shape((2, EDGE + PAD, MIXED), F32),
            shape((HEADS, 2 * BLOCK), F32),
        ],
        [pltpu.VMEM((2, TILES, PAD + BLOCK, 128), F32)],
        [across, *shared],
        10**9,
        12,
    )
    others = [mask for mask in range(1, count) if mask != top]
    (out,) = call(
        functools.partial(join_kernel, count, top),
        "join_blocks",
        [shape((BLOCK, EMBED), BF16)],
        [
            pltpu.VMEM((2 * len(others) * BLOCK, EMBED), BF16),
            pltpu.VMEM((2 * len(others), TILES, PAD + BLOCK, 128), F32),
            pltpu.VMEM((4, 2 * N, E), BF16),
            pltpu.VMEM((4, PAD + EDGE, MIXED), F32),
            pltpu.VMEM((2, TILES, PAD + EDGE, 128), F32),
            pltpu.VMEM((4, BLOCK, E), F32),
        ],
        [
            *[received[mask] for mask in others],
            *shared,
            row(skip_gain),
            row(gate_gain),
            output_weight,
            decay,
            lift,
            *own,
            *ahead,
        ],
        2 * 10**9,
        18 + 2 * len(others),
    )
    return out


def solution(mesh):
    in_specs = (P(("batch", "seq"), None), P(), P(), P(), P(), P(), P(), P(), P(), P(), P())
    out_specs = P(("batch", "seq"), None)
    return jax.shard_map(
        on_device, mesh=mesh, in_specs=in_specs, out_specs=out_specs, check_vma=False
    )
```

```python
import functools

import jax
import jax.numpy as jnp
from jax import lax
from jax.experimental import pallas as pl
from jax.experimental.pallas import tpu as pltpu
from jax.sharding import PartitionSpec as P

EMBED = 512
E = 1024
N = 64
K = 4
BLOCK = 128
HEADS = 16
MIXED = E + 2 * N
TILES = MIXED // 128
PAIRS = E // 128
GROUPS = EMBED // 128
PAD = 8
EDGE = 16
UPFRONT = 4
eps = 1e-05
F32 = jnp.float32
BF16 = jnp.bfloat16


def dot(a, b):
    return jnp.dot(a, b, preferred_element_type=F32)


def dot_rows(a, b):
    return lax.dot_general(a, b, (((1,), (1,)), ((), ())), preferred_element_type=F32)


def iota(shape, axis):
    return lax.broadcasted_iota(jnp.int32, shape, axis)


def reversal():
    return (iota((128, 128), 0) + iota((128, 128), 1) == 127).astype(BF16)


def split(values, terms):
    parts = []
    for _ in range(terms):
        part = values.astype(BF16)
        parts.append(part)
        values = values - part.astype(F32)
    return parts


def exact_dot(values, mask):
    return sum(dot(part, mask) for part in split(values, 3))


def flip_lanes(rows, swap):
    return jnp.concatenate(
        [dot(rows[:, 128 * (GROUPS - 1 - g) : 128 * (GROUPS - g)], swap) for g in range(GROUPS)],
        axis=1,
    )


def both_normed(rows, gain, swap):
    floats = rows.astype(F32)
    scale = lax.rsqrt(jnp.mean(floats * floats, axis=-1, keepdims=True) + eps)
    flipped = flip_lanes(rows.astype(BF16), swap)
    return [(floats * scale * gain).astype(BF16), (flipped * scale * gain).astype(BF16)]


def half_silu(half):
    return half + half * jnp.tanh(half)


def column_of(row):
    shape = (HEADS, HEADS)
    return jnp.sum(
        jnp.where(iota(shape, 0) == iota(shape, 1), row, 0.0), axis=1, keepdims=True
    )


def log_decays(step_raw, step_bias, log_rate):
    v = step_raw + column_of(step_bias)
    u = jnp.exp(-jnp.abs(v))
    series = 1.0 / 7.0
    for order in range(6, 0, -1):
        series = 1.0 / order - u * series
    rest = jnp.where(u < 0.0625, u * series, jnp.log(1.0 + u))
    return -jnp.exp(column_of(log_rate)) * (jnp.maximum(v, 0.0) + rest)


def selectors(terms, heads):
    shape = (terms * HEADS, 256)
    head = iota(shape, 0) & (HEADS - 1)
    near = iota(shape, 1) >> (8 - (heads.bit_length() - 1))
    return [(head - near == low).astype(BF16) for low in range(0, HEADS, heads)]


def stacked_split(values, terms):
    return jnp.concatenate(split(values, terms), axis=0)


def dot_columns(a, b):
    return lax.dot_general(a, b, (((0,), (0,)), ((), ())), preferred_element_type=F32)


def lanes_of(tile):
    return slice(tile * 128, tile * 128 + 128)


def chunks(width):
    return [(start, min(start + 256, width)) for start in range(0, width, 256)]


def filtered(source, at, lanes, taps, bias, backward=False, rows=BLOCK):
    result = bias[:, lanes]
    for k in range(K):
        low = at + ((K - 1) - k if backward else k - (K - 1))
        result = result + taps[k : k + 1, lanes] * source[low : low + rows]
    return result


def own_kernel(*refs):
    sources, refs = refs[:8], refs[8:]
    (decay_ref, lift_ref, activated_ref, edge_ref, silu_gate_ref), refs = refs[:5], refs[5:]
    held, (x_ref, extended_ref, semaphores) = refs[:7], refs[7:]
    copies = [
        pltpu.make_async_copy(source, target, semaphores.at[place])
        for place, (source, target) in enumerate(zip(sources, (x_ref, *held)))
    ]
    for copy in copies:
        copy.start()
    norm_gain_ref, step_weight_ref, step_bias_ref, log_rate_ref = held[:4]
    input_weight_ref, conv_weight_ref, conv_bias_ref = held[4:]
    for copy in copies[:5]:
        copy.wait()
    normal = jnp.concatenate(both_normed(x_ref[...], norm_gain_ref[...], reversal()), axis=0)
    log_decay = log_decays(
        dot_rows(step_weight_ref[...], normal), step_bias_ref[...], log_rate_ref[...]
    )
    row, column = iota((BLOCK, BLOCK), 0), iota((BLOCK, BLOCK), 1)
    lower = row >= column
    both = jnp.concatenate([log_decay[:, :BLOCK], log_decay[:, BLOCK:]], axis=0)
    before = exact_dot(both, (row <= column).astype(BF16))
    after = exact_dot(both, (row >= column).astype(BF16))
    twos, fours = selectors(3, 2), selectors(1, 4)
    ones = jnp.ones((3 * HEADS, BLOCK), BF16)

    def sides_of(rows):
        parts = stacked_split(rows, 3)
        return jnp.concatenate([parts, ones], axis=0), jnp.concatenate([-parts] * 2, axis=1)

    heads = [slice(flip * HEADS, (flip + 1) * HEADS) for flip in range(2)]
    sides = [[sides_of(rows[heads[flip]]) for rows in (before, after)] for flip in range(2)]
    lifts = [[jnp.exp(rows[heads[flip]]).astype(BF16) for rows in (before, after)] for flip in range(2)]

    def put_decay(flip, pair):
        spreads = [
            dot_columns(plus, jnp.concatenate([twos[pair], twos[pair] * minus], axis=0))
            for plus, minus in sides[flip]
        ]
        for near in range(2):
            lanes = lanes_of(near)
            decay_ref[flip, 2 * pair + near] = jnp.exp(
                jnp.where(lower, spreads[0][:, lanes], spreads[1][:, lanes])
            ).astype(BF16)

    def put_lift(flip, way, place):
        start, stop = chunks(E)[place]
        lift_ref[2 * flip + way, :, start:stop] = dot_columns(
            lifts[flip][way], fours[place]
        ).astype(BF16)

    spare = [functools.partial(put_decay, flip, pair) for flip in range(2) for pair in range(PAIRS)]
    spare += [
        functools.partial(put_lift, flip, way, place)
        for flip in range(2)
        for way in range(2)
        for place in range(PAIRS // 2)
    ]
    for _ in range(UPFRONT):
        spare.pop(0)()
    for copy in copies[5:]:
        copy.wait()
    taps, bias = 0.5 * conv_weight_ref[...], 0.5 * conv_bias_ref[...].reshape(1, MIXED)
    for start, stop in chunks(MIXED):
        mixed = dot(normal, input_weight_ref[:, E + start : E + stop])
        for flip in range(2):
            rows = mixed[flip * BLOCK : (flip + 1) * BLOCK]
            edge_ref[flip, :EDGE, start:stop] = rows[:EDGE]
            edge_ref[flip, EDGE:, start:stop] = rows[BLOCK - EDGE :]
            for tile in range(start // 128, stop // 128):
                lanes = lanes_of(tile)
                place = extended_ref.at[flip, tile]
                place[:PAD] = jnp.zeros((PAD, 128), F32)
                place[PAD + BLOCK :] = jnp.zeros((PAD, 128), F32)
                place[PAD : PAD + BLOCK] = rows[:, tile * 128 - start : tile * 128 - start + 128]
        for flip in range(2):
            for tile in range(start // 128, stop // 128):
                lanes = lanes_of(tile)
                place = extended_ref.at[flip, tile]
                for way in range(2):
                    if spare:
                        spare.pop(0)()
                    half = filtered(place, PAD, lanes, taps, bias, way == 1)
                    activated_ref[2 * flip + way, :, lanes] = half_silu(half).astype(BF16)
    for start, stop in chunks(E):
        gate = dot(normal, input_weight_ref[:, start:stop])
        if spare:
            spare.pop(0)()
        gate = half_silu(0.5 * gate)
        for flip in range(2):
            silu_gate_ref[flip, :, start:stop] = gate[flip * BLOCK : (flip + 1) * BLOCK]
    for left_over in spare:
        left_over()


def chain_rows(mask, index, block, gain, swap):
    row, column = iota((BLOCK, BLOCK), 0), iota((BLOCK, BLOCK), 1)
    order = jnp.where((index ^ mask) < index, row, 127 - row) == column
    return both_normed(dot(order.astype(BF16), block), gain, swap)


def ahead_kernel(
    mask,
    block_ref,
    norm_gain_ref,
    input_weight_ref,
    step_weight_ref,
    conv_weight_ref,
    conv_bias_ref,
    step_bias_ref,
    log_rate_ref,
    activated_ref,
    edge_ref,
    log_decay_ref,
    extended_ref,
):
    index = lax.axis_index("seq")
    normal = jnp.concatenate(
        chain_rows(mask, index, block_ref[...], norm_gain_ref[...], reversal()), axis=0
    )
    log_decay_ref[...] = log_decays(
        dot_rows(step_weight_ref[...], normal), step_bias_ref[...], log_rate_ref[...]
    )
    taps, bias = 0.5 * conv_weight_ref[...], 0.5 * conv_bias_ref[...].reshape(1, MIXED)
    for start, stop in chunks(MIXED):
        mixed = dot(normal, input_weight_ref[:, E + start : E + stop])
        for flip in range(2):
            rows = mixed[flip * BLOCK : (flip + 1) * BLOCK]
            edge_ref[flip, :EDGE, start:stop] = rows[:EDGE]
            edge_ref[flip, EDGE:, start:stop] = rows[BLOCK - PAD :]
            for tile in range(start // 128, stop // 128):
                lanes = lanes_of(tile)
                place = extended_ref.at[flip, tile]
                place[:PAD] = jnp.zeros((PAD, 128), F32)
                place[PAD:] = rows[:, tile * 128 - start : tile * 128 - start + 128]
                half = filtered(place, PAD, lanes, taps, bias)
                activated_ref[flip, :, lanes] = half_silu(half).astype(BF16)


def join_kernel(count, top, *refs):
    others = [mask for mask in range(1, count) if mask != top]
    received, refs = refs[: len(others)], refs[len(others) :]
    (
        norm_gain_ref,
        input_weight_ref,
        step_weight_ref,
        conv_weight_ref,
        conv_bias_ref,
        step_bias_ref,
        log_rate_ref,
        skip_gain_ref,
        gate_gain_ref,
        output_weight_ref,
        decay_ref,
        lift_ref,
        activated_ref,
        edge_ref,
        silu_gate_ref,
        ahead_ref,
        ahead_edge_ref,
        ahead_log_decay_ref,
        out_ref,
        normal_ref,
        extended_ref,
        memory_ref,
        window_ref,
        patch_ref,
        gated_ref,
    ) = refs
    index = lax.axis_index("seq")
    swap = reversal()
    row, column = iota((BLOCK, BLOCK), 0), iota((BLOCK, BLOCK), 1)
    lower, upper = row >= column, row <= column
    left, right = (column < N).astype(BF16), (column >= N).astype(BF16)
    taps, bias = 0.5 * conv_weight_ref[...], 0.5 * conv_bias_ref[...].reshape(1, MIXED)

    def picked(rows, block):
        result = jnp.zeros((PAD, rows[top].shape[1]), F32)
        for mask, part in rows.items():
            result = jnp.where((index ^ mask) == block, part, result)
        return result

    for place, mask in enumerate(others):
        block = received[place][...]
        for flip, part in enumerate(chain_rows(mask, index, block, norm_gain_ref[...], swap)):
            low = (2 * place + flip) * BLOCK
            normal_ref[low : low + BLOCK] = part
    normal = normal_ref[...]
    log_decay = log_decays(
        dot_rows(step_weight_ref[...], normal), step_bias_ref[...], log_rate_ref[...]
    )
    pieces = {}
    for flip in range(2):
        for place, mask in enumerate(others):
            low = (2 * place + flip) * BLOCK
            pieces[mask, flip] = log_decay[:, low : low + BLOCK]
        pieces[top, flip] = ahead_log_decay_ref[:, flip * BLOCK : (flip + 1) * BLOCK]
    parts = [(mask, flip) for mask in range(1, count) for flip in range(2)]
    tails = exact_dot(
        jnp.concatenate([pieces[part] for part in parts], axis=0), (row > column).astype(BF16)
    )
    wholes = {part: jnp.sum(pieces[part], axis=1, keepdims=True) for part in parts}
    faded = [[], []]
    for at, (mask, flip) in enumerate(parts):
        tail = tails[at * HEADS : (at + 1) * HEADS]
        block = index ^ mask
        for other in range(1, count):
            if other != mask:
                between = index ^ other
                later = ((block < between) & (between < index)) | (
                    (index < between) & (between < block)
                )
                tail = tail + jnp.where(later, wholes[other, flip], 0.0)
        faded[flip].append(jnp.exp(tail))
    faded = [jnp.concatenate(rows, axis=1).astype(BF16) for rows in faded]
    fours = selectors(1, 4)

    writers = [None, None]
    order = chunks(MIXED)
    order = order[-1:] + order[:-1]

    def project(place):
        start, stop = order[place]
        return dot(normal, input_weight_ref[:, E + start : E + stop])

    def fade_of(place, flip):
        return dot_columns(faded[flip], fours[order[place][0] // 256]).astype(BF16)

    ready, coming = project(0), None
    for turn, (start, stop) in enumerate(order):
        mixed = ready
        if turn + 1 < len(order):
            ready = project(turn + 1)
            fades, coming = coming, [fade_of(turn + 1, flip) for flip in range(2)]
        else:
            fades = coming
        for flip in range(2):
            acted, last = {}, {top: ahead_edge_ref[flip, EDGE:, start:stop]}
            for place, mask in enumerate(others):
                low = (2 * place + flip) * BLOCK
                last[mask] = mixed[low + BLOCK - PAD : low + BLOCK]
            window_ref[2 * flip, :PAD, start:stop] = picked(last, index - 1)
            behind = picked(last, index + 1)
            for step in range(K - 1):
                spot = slice(EDGE + step, EDGE + step + 1)
                window_ref[2 * flip + 1, spot, start:stop] = behind[PAD - 1 - step : PAD - step]
            for mask in range(1, count):
                block = index ^ mask
                halo = picked(last, jnp.where(block < index, block - 1, block + 1))
                if mask == top:
                    near = []
                    for tile in range(start // 128, stop // 128):
                        lanes = lanes_of(tile)
                        spot = patch_ref.at[flip, tile]
                        spot[:PAD] = halo[:, tile * 128 - start : tile * 128 - start + 128]
                        spot[PAD:] = ahead_edge_ref[flip, :EDGE, lanes]
                        half = filtered(spot, PAD, lanes, taps, bias, False, EDGE)
                        patch = half_silu(half).astype(BF16)
                        near.append(
                            jnp.concatenate([patch, ahead_ref[flip, EDGE:, lanes]], axis=0)
                        )
                    acted[mask] = jnp.concatenate(near, axis=1)
                    continue
                place = others.index(mask)
                low = (2 * place + flip) * BLOCK
                near = []
                for tile in range(start // 128, stop // 128):
                    at = tile * 128 - start
                    spot = extended_ref.at[2 * place + flip, tile]
                    spot[:PAD] = halo[:, at : at + 128]
                    spot[PAD:] = mixed[low : low + BLOCK, at : at + 128]
                    half = filtered(spot, PAD, lanes_of(tile), taps, bias)
                    near.append(half_silu(half).astype(BF16))
                acted[mask] = jnp.concatenate(near, axis=1)
            if start == E:
                sides = []
                for mask in range(1, count):
                    maps = acted[mask].T[:N]
                    earlier = jnp.where((index ^ mask) < index, 1.0, 0.0).astype(BF16)
                    later = jnp.where((index ^ mask) < index, 0.0, 1.0).astype(BF16)
                    sides.append(jnp.concatenate([maps * earlier, maps * later], axis=0))
                writers[flip] = jnp.concatenate(sides, axis=1)
                continue
            fade = fades[flip]
            decayed = [
                fade[at * BLOCK : (at + 1) * BLOCK] * acted[at + 1]
                for at in range(count - 1)
            ]
            memory = dot(writers[flip], jnp.concatenate(decayed, axis=0))
            for way in range(2):
                kept = memory[way * N : (way + 1) * N]
                even = (iota(kept.shape, 1) & N) == 0
                chain = 2 * flip + way
                memory_ref[chain, :N, start:stop] = jnp.where(even, kept, 0.0).astype(BF16)
                memory_ref[chain, N:, start:stop] = jnp.where(even, 0.0, kept).astype(BF16)

    skip = wide_row(skip_gain_ref[...])
    for flip in range(2):
        for way in range(2):
            chain = 2 * flip + way
            spot = window_ref.at[chain]
            if way == 0:
                spot[PAD:] = edge_ref[flip, :EDGE]
            else:
                spot[:EDGE] = edge_ref[flip, EDGE:]
            at = PAD if way == 0 else 0
            half = filtered(spot, at, slice(0, MIXED), taps, bias, way == 1, EDGE)
            patch = half_silu(half).astype(BF16)

            def acted(tile):
                lanes = lanes_of(tile)
                if way == 0:
                    near = [patch[:, lanes], activated_ref[chain, EDGE:, lanes]]
                else:
                    near = [activated_ref[chain, : BLOCK - EDGE, lanes], patch[:, lanes]]
                return jnp.concatenate(near, axis=0)

            maps = acted(PAIRS)
            writer, reader = maps[:, :N], maps[:, N:]
            scores = jnp.where(lower if way == 0 else upper, dot_rows(reader, writer), 0.0)
            scores = scores.astype(BF16)
            squares = jnp.zeros((BLOCK, 128), F32)
            doubled = jnp.concatenate([reader, reader], axis=1)
            for pair in range(PAIRS):
                lanes = lanes_of(pair)
                signal = acted(pair)
                signals = jnp.concatenate(
                    [signal * left, signal * right, memory_ref[chain, :, lanes]], axis=0
                )
                weights = jnp.concatenate(
                    [
                        decay_ref[flip, 2 * pair + near] * scores
                        for near in range(2)
                    ]
                    + [lift_ref[chain, :, lanes] * doubled],
                    axis=1,
                )
                inside = dot(weights, signals)
                gated = inside + skip[:, lanes] * signal.astype(F32)
                gated = gated * silu_gate_ref[flip, :, lanes]
                squares = squares + gated * gated
                gated_ref[chain, :, lanes] = gated
            scale = lax.rsqrt(jnp.sum(squares, axis=1, keepdims=True) * (1.0 / E) + eps)
            for pair in range(PAIRS):
                lanes = lanes_of(pair)
                gated_ref[chain, :, lanes] = (
                    gated_ref[chain, :, lanes] * scale * gate_gain_ref[:, lanes]
                )

    normed = gated_ref[...].astype(BF16).reshape(4 * BLOCK, E)
    made = dot(normed, output_weight_ref[...])
    straight, crossed = made[: 2 * BLOCK], made[2 * BLOCK :]
    high, low = split(crossed, 2)
    both = straight + flip_lanes(high, swap) + flip_lanes(low, swap)
    backward = both[BLOCK:].astype(BF16).astype(F32)
    out_ref[...] = (both[:BLOCK] + backward).astype(BF16)


def wide_row(row):
    select = (iota((HEADS, E), 1) // N == iota((HEADS, E), 0)).astype(BF16)
    return exact_dot(jnp.broadcast_to(row, (8, HEADS)), select)[:1]


def swapped(rows, step, count):
    return lax.ppermute(rows, "seq", [(i, i ^ step) for i in range(count)])


def on_device(
    hidden,
    norm_gain,
    input_weight,
    step_weight,
    conv_weight,
    conv_bias,
    step_bias,
    log_rate,
    skip_gain,
    gate_gain,
    output_weight,
):
    count = lax.axis_size("seq")
    top = count // 2
    row = lambda vector: vector.reshape(1, -1)
    whole = pl.BlockSpec(memory_space=pltpu.VMEM)
    shape = jax.ShapeDtypeStruct
    gain, step_map = row(norm_gain), step_weight.T
    step_bias, log_rate = row(step_bias), row(log_rate)
    across = swapped(hidden, top, count)

    def call(kernel, name, outs, scratch, operands, flops, limit, spec=whole):
        return pl.pallas_call(
            kernel,
            out_shape=outs,
            in_specs=[spec] * len(operands),
            out_specs=[whole] * len(outs),
            scratch_shapes=scratch,
            compiler_params=pltpu.CompilerParams(vmem_limit_bytes=limit * 2**20),
            cost_estimate=pl.CostEstimate(
                flops=flops, bytes_accessed=10**7, transcendentals=10**6
            ),
            name=name,
        )(*operands)

    operands = (
        hidden, gain, step_map, step_bias, log_rate, input_weight, conv_weight, conv_bias
    )
    made = call(
        own_kernel,
        "own_rows",
        [
            shape((2, HEADS, BLOCK, BLOCK), BF16),
            shape((4, BLOCK, E), BF16),
            shape((4, BLOCK, MIXED), BF16),
            shape((2, 2 * EDGE, MIXED), F32),
            shape((2, BLOCK, E), F32),
            *[shape(part.shape, part.dtype) for part in operands[1:]],
        ],
        [
            pltpu.VMEM(hidden.shape, hidden.dtype),
            pltpu.VMEM((2, TILES, BLOCK + 2 * PAD, 128), F32),
            pltpu.SemaphoreType.DMA((8,)),
        ],
        [pltpu.with_memory_space_constraint(part, pltpu.HBM) for part in operands],
        2 * 10**9,
        24,
        pl.BlockSpec(memory_space=pltpu.HBM),
    )
    decay, lift, *own = made[:5]
    gain, step_map, step_bias, log_rate, input_weight, conv_weight, conv_bias = made[5:]
    start, across, decay, lift, *own = lax.optimization_barrier(
        (hidden, across, decay, lift, *own)
    )
    received = {0: start, top: across}
    for bit in reversed(range(top.bit_length() - 1)):
        for mask in sorted(received):
            received[mask | 1 << bit] = swapped(received[mask], 1 << bit, count)
    shared = [gain, input_weight, step_map, conv_weight, conv_bias, step_bias, log_rate]
    ahead = call(
        functools.partial(ahead_kernel, top),
        "across_rows",
        [
            shape((2, BLOCK, MIXED), BF16),
            shape((2, EDGE + PAD, MIXED), F32),
            shape((HEADS, 2 * BLOCK), F32),
        ],
        [pltpu.VMEM((2, TILES, PAD + BLOCK, 128), F32)],
        [across, *shared],
        10**9,
        12,
    )
    others = [mask for mask in range(1, count) if mask != top]
    (out,) = call(
        functools.partial(join_kernel, count, top),
        "join_blocks",
        [shape((BLOCK, EMBED), BF16)],
        [
            pltpu.VMEM((2 * len(others) * BLOCK, EMBED), BF16),
            pltpu.VMEM((2 * len(others), TILES, PAD + BLOCK, 128), F32),
            pltpu.VMEM((4, 2 * N, E), BF16),
            pltpu.VMEM((4, PAD + EDGE, MIXED), F32),
            pltpu.VMEM((2, TILES, PAD + EDGE, 128), F32),
            pltpu.VMEM((4, BLOCK, E), F32),
        ],
        [
            *[received[mask] for mask in others],
            *shared,
            row(skip_gain),
            row(gate_gain),
            output_weight,
            decay,
            lift,
            *own,
            *ahead,
        ],
        2 * 10**9,
        18 + 2 * len(others),
    )
    return out


def solution(mesh):
    in_specs = (P(("batch", "seq"), None), P(), P(), P(), P(), P(), P(), P(), P(), P(), P())
    out_specs = P(("batch", "seq"), None)
    return jax.shard_map(
        on_device, mesh=mesh, in_specs=in_specs, out_specs=out_specs, check_vma=False
    )
```

```python
import functools

import jax
import jax.numpy as jnp
from jax import lax
from jax.experimental import pallas as pl
from jax.experimental.pallas import tpu as pltpu
from jax.sharding import PartitionSpec as P

EMBED = 512
E = 1024
N = 64
K = 4
BLOCK = 128
HEADS = 16
MIXED = E + 2 * N
TILES = MIXED // 128
PAIRS = E // 128
GROUPS = EMBED // 128
PAD = 8
EDGE = 16
UPFRONT = 4
eps = 1e-05
F32 = jnp.float32
BF16 = jnp.bfloat16


def dot(a, b):
    return jnp.dot(a, b, preferred_element_type=F32)


def dot_rows(a, b):
    return lax.dot_general(a, b, (((1,), (1,)), ((), ())), preferred_element_type=F32)


def iota(shape, axis):
    return lax.broadcasted_iota(jnp.int32, shape, axis)


def reversal():
    return (iota((128, 128), 0) + iota((128, 128), 1) == 127).astype(BF16)


def split(values, terms):
    parts = []
    for _ in range(terms):
        part = values.astype(BF16)
        parts.append(part)
        values = values - part.astype(F32)
    return parts


def exact_dot(values, mask):
    return sum(dot(part, mask) for part in split(values, 3))


def flip_lanes(rows, swap):
    return jnp.concatenate(
        [dot(rows[:, 128 * (GROUPS - 1 - g) : 128 * (GROUPS - g)], swap) for g in range(GROUPS)],
        axis=1,
    )


def both_normed(rows, gain, swap):
    floats = rows.astype(F32)
    scale = lax.rsqrt(jnp.mean(floats * floats, axis=-1, keepdims=True) + eps)
    flipped = flip_lanes(rows.astype(BF16), swap)
    return [(floats * scale * gain).astype(BF16), (flipped * scale * gain).astype(BF16)]


def half_silu(half):
    return half + half * jnp.tanh(half)


def column_of(row):
    shape = (HEADS, HEADS)
    return jnp.sum(
        jnp.where(iota(shape, 0) == iota(shape, 1), row, 0.0), axis=1, keepdims=True
    )


def log_decays(step_raw, step_bias, log_rate):
    v = step_raw + column_of(step_bias)
    u = jnp.exp(-jnp.abs(v))
    series = 1.0 / 7.0
    for order in range(6, 0, -1):
        series = 1.0 / order - u * series
    rest = jnp.where(u < 0.0625, u * series, jnp.log(1.0 + u))
    return -jnp.exp(column_of(log_rate)) * (jnp.maximum(v, 0.0) + rest)


def selectors(terms, heads):
    shape = (terms * HEADS, 256)
    head = iota(shape, 0) & (HEADS - 1)
    near = iota(shape, 1) >> (8 - (heads.bit_length() - 1))
    return [(head - near == low).astype(BF16) for low in range(0, HEADS, heads)]


def stacked_split(values, terms):
    return jnp.concatenate(split(values, terms), axis=0)


def dot_columns(a, b):
    return lax.dot_general(a, b, (((0,), (0,)), ((), ())), preferred_element_type=F32)


def lanes_of(tile):
    return slice(tile * 128, tile * 128 + 128)


def chunks(width):
    return [(start, min(start + 256, width)) for start in range(0, width, 256)]


def filtered(source, at, lanes, taps, bias, backward=False, rows=BLOCK):
    result = bias[:, lanes]
    for k in range(K):
        low = at + ((K - 1) - k if backward else k - (K - 1))
        result = result + taps[k : k + 1, lanes] * source[low : low + rows]
    return result


def own_kernel(
    opening_ref,
    x_ref,
    norm_gain_ref,
    step_weight_ref,
    step_bias_ref,
    log_rate_ref,
    input_weight_ref,
    conv_weight_ref,
    conv_bias_ref,
    decay_ref,
    lift_ref,
    activated_ref,
    edge_ref,
    silu_gate_ref,
    extended_ref,
):
    normal = jnp.concatenate(both_normed(x_ref[...], norm_gain_ref[...], reversal()), axis=0)
    log_decay = log_decays(
        dot_rows(step_weight_ref[...], normal), step_bias_ref[...], log_rate_ref[...]
    )
    row, column = iota((BLOCK, BLOCK), 0), iota((BLOCK, BLOCK), 1)
    lower = row >= column
    both = jnp.concatenate([log_decay[:, :BLOCK], log_decay[:, BLOCK:]], axis=0)
    before = exact_dot(both, (row <= column).astype(BF16))
    after = exact_dot(both, (row >= column).astype(BF16))
    twos, fours = selectors(3, 2), selectors(1, 4)
    ones = jnp.ones((3 * HEADS, BLOCK), BF16)

    def sides_of(rows):
        parts = stacked_split(rows, 3)
        return jnp.concatenate([parts, ones], axis=0), jnp.concatenate([-parts] * 2, axis=1)

    heads = [slice(flip * HEADS, (flip + 1) * HEADS) for flip in range(2)]
    sides = [[sides_of(rows[heads[flip]]) for rows in (before, after)] for flip in range(2)]
    lifts = [[jnp.exp(rows[heads[flip]]).astype(BF16) for rows in (before, after)] for flip in range(2)]

    def put_decay(flip, pair):
        spreads = [
            dot_columns(plus, jnp.concatenate([twos[pair], twos[pair] * minus], axis=0))
            for plus, minus in sides[flip]
        ]
        for near in range(2):
            lanes = lanes_of(near)
            decay_ref[flip, 2 * pair + near] = jnp.exp(
                jnp.where(lower, spreads[0][:, lanes], spreads[1][:, lanes])
            ).astype(BF16)

    def put_lift(flip, way, place):
        start, stop = chunks(E)[place]
        lift_ref[2 * flip + way, :, start:stop] = dot_columns(
            lifts[flip][way], fours[place]
        ).astype(BF16)

    spare = [functools.partial(put_decay, flip, pair) for flip in range(2) for pair in range(PAIRS)]
    spare += [
        functools.partial(put_lift, flip, way, place)
        for flip in range(2)
        for way in range(2)
        for place in range(PAIRS // 2)
    ]
    for _ in range(UPFRONT):
        spare.pop(0)()
    taps, bias = 0.5 * conv_weight_ref[...], 0.5 * conv_bias_ref[...].reshape(1, MIXED)
    for start, stop in chunks(MIXED):
        mixed = dot(normal, input_weight_ref[:, E + start : E + stop])
        for flip in range(2):
            rows = mixed[flip * BLOCK : (flip + 1) * BLOCK]
            edge_ref[flip, :EDGE, start:stop] = rows[:EDGE]
            edge_ref[flip, EDGE:, start:stop] = rows[BLOCK - EDGE :]
            for tile in range(start // 128, stop // 128):
                lanes = lanes_of(tile)
                place = extended_ref.at[flip, tile]
                place[:PAD] = jnp.zeros((PAD, 128), F32)
                place[PAD + BLOCK :] = jnp.zeros((PAD, 128), F32)
                place[PAD : PAD + BLOCK] = rows[:, tile * 128 - start : tile * 128 - start + 128]
        for flip in range(2):
            for tile in range(start // 128, stop // 128):
                lanes = lanes_of(tile)
                place = extended_ref.at[flip, tile]
                for way in range(2):
                    if spare:
                        spare.pop(0)()
                    half = filtered(place, PAD, lanes, taps, bias, way == 1)
                    activated_ref[2 * flip + way, :, lanes] = half_silu(half).astype(BF16)
    for start, stop in chunks(E):
        gate = dot(normal, input_weight_ref[:, start:stop])
        if spare:
            spare.pop(0)()
        gate = half_silu(0.5 * gate)
        for flip in range(2):
            silu_gate_ref[flip, :, start:stop] = gate[flip * BLOCK : (flip + 1) * BLOCK]
    for left_over in spare:
        left_over()


def chain_rows(mask, index, block, gain, swap):
    row, column = iota((BLOCK, BLOCK), 0), iota((BLOCK, BLOCK), 1)
    order = jnp.where((index ^ mask) < index, row, 127 - row) == column
    return both_normed(dot(order.astype(BF16), block), gain, swap)


def ahead_kernel(
    mask,
    block_ref,
    norm_gain_ref,
    input_weight_ref,
    step_weight_ref,
    conv_weight_ref,
    conv_bias_ref,
    step_bias_ref,
    log_rate_ref,
    activated_ref,
    edge_ref,
    log_decay_ref,
    extended_ref,
):
    index = lax.axis_index("seq")
    normal = jnp.concatenate(
        chain_rows(mask, index, block_ref[...], norm_gain_ref[...], reversal()), axis=0
    )
    log_decay_ref[...] = log_decays(
        dot_rows(step_weight_ref[...], normal), step_bias_ref[...], log_rate_ref[...]
    )
    taps, bias = 0.5 * conv_weight_ref[...], 0.5 * conv_bias_ref[...].reshape(1, MIXED)
    for start, stop in chunks(MIXED):
        mixed = dot(normal, input_weight_ref[:, E + start : E + stop])
        for flip in range(2):
            rows = mixed[flip * BLOCK : (flip + 1) * BLOCK]
            edge_ref[flip, :EDGE, start:stop] = rows[:EDGE]
            edge_ref[flip, EDGE:, start:stop] = rows[BLOCK - PAD :]
            for tile in range(start // 128, stop // 128):
                lanes = lanes_of(tile)
                place = extended_ref.at[flip, tile]
                place[:PAD] = jnp.zeros((PAD, 128), F32)
                place[PAD:] = rows[:, tile * 128 - start : tile * 128 - start + 128]
                half = filtered(place, PAD, lanes, taps, bias)
                activated_ref[flip, :, lanes] = half_silu(half).astype(BF16)


def join_kernel(count, top, *refs):
    others = [mask for mask in range(1, count) if mask != top]
    received, refs = refs[: len(others)], refs[len(others) :]
    (
        norm_gain_ref,
        input_weight_ref,
        step_weight_ref,
        conv_weight_ref,
        conv_bias_ref,
        step_bias_ref,
        log_rate_ref,
        skip_gain_ref,
        gate_gain_ref,
        output_weight_ref,
        decay_ref,
        lift_ref,
        activated_ref,
        edge_ref,
        silu_gate_ref,
        ahead_ref,
        ahead_edge_ref,
        ahead_log_decay_ref,
        out_ref,
        normal_ref,
        extended_ref,
        memory_ref,
        window_ref,
        patch_ref,
        gated_ref,
    ) = refs
    index = lax.axis_index("seq")
    swap = reversal()
    row, column = iota((BLOCK, BLOCK), 0), iota((BLOCK, BLOCK), 1)
    lower, upper = row >= column, row <= column
    left, right = (column < N).astype(BF16), (column >= N).astype(BF16)
    taps, bias = 0.5 * conv_weight_ref[...], 0.5 * conv_bias_ref[...].reshape(1, MIXED)

    def picked(rows, block):
        result = jnp.zeros((PAD, rows[top].shape[1]), F32)
        for mask, part in rows.items():
            result = jnp.where((index ^ mask) == block, part, result)
        return result

    for place, mask in enumerate(others):
        block = received[place][...]
        for flip, part in enumerate(chain_rows(mask, index, block, norm_gain_ref[...], swap)):
            low = (2 * place + flip) * BLOCK
            normal_ref[low : low + BLOCK] = part
    normal = normal_ref[...]
    log_decay = log_decays(
        dot_rows(step_weight_ref[...], normal), step_bias_ref[...], log_rate_ref[...]
    )
    pieces = {}
    for flip in range(2):
        for place, mask in enumerate(others):
            low = (2 * place + flip) * BLOCK
            pieces[mask, flip] = log_decay[:, low : low + BLOCK]
        pieces[top, flip] = ahead_log_decay_ref[:, flip * BLOCK : (flip + 1) * BLOCK]
    parts = [(mask, flip) for mask in range(1, count) for flip in range(2)]
    tails = exact_dot(
        jnp.concatenate([pieces[part] for part in parts], axis=0), (row > column).astype(BF16)
    )
    wholes = {part: jnp.sum(pieces[part], axis=1, keepdims=True) for part in parts}
    faded = [[], []]
    for at, (mask, flip) in enumerate(parts):
        tail = tails[at * HEADS : (at + 1) * HEADS]
        block = index ^ mask
        for other in range(1, count):
            if other != mask:
                between = index ^ other
                later = ((block < between) & (between < index)) | (
                    (index < between) & (between < block)
                )
                tail = tail + jnp.where(later, wholes[other, flip], 0.0)
        faded[flip].append(jnp.exp(tail))
    faded = [jnp.concatenate(rows, axis=1).astype(BF16) for rows in faded]
    fours = selectors(1, 4)

    writers = [None, None]
    order = chunks(MIXED)
    order = order[-1:] + order[:-1]

    def project(place):
        start, stop = order[place]
        return dot(normal, input_weight_ref[:, E + start : E + stop])

    def fade_of(place, flip):
        return dot_columns(faded[flip], fours[order[place][0] // 256]).astype(BF16)

    ready, coming = project(0), None
    for turn, (start, stop) in enumerate(order):
        mixed = ready
        if turn + 1 < len(order):
            ready = project(turn + 1)
            fades, coming = coming, [fade_of(turn + 1, flip) for flip in range(2)]
        else:
            fades = coming
        for flip in range(2):
            acted, last = {}, {top: ahead_edge_ref[flip, EDGE:, start:stop]}
            for place, mask in enumerate(others):
                low = (2 * place + flip) * BLOCK
                last[mask] = mixed[low + BLOCK - PAD : low + BLOCK]
            window_ref[2 * flip, :PAD, start:stop] = picked(last, index - 1)
            behind = picked(last, index + 1)
            for step in range(K - 1):
                spot = slice(EDGE + step, EDGE + step + 1)
                window_ref[2 * flip + 1, spot, start:stop] = behind[PAD - 1 - step : PAD - step]
            for mask in range(1, count):
                block = index ^ mask
                halo = picked(last, jnp.where(block < index, block - 1, block + 1))
                if mask == top:
                    near = []
                    for tile in range(start // 128, stop // 128):
                        lanes = lanes_of(tile)
                        spot = patch_ref.at[flip, tile]
                        spot[:PAD] = halo[:, tile * 128 - start : tile * 128 - start + 128]
                        spot[PAD:] = ahead_edge_ref[flip, :EDGE, lanes]
                        half = filtered(spot, PAD, lanes, taps, bias, False, EDGE)
                        patch = half_silu(half).astype(BF16)
                        near.append(
                            jnp.concatenate([patch, ahead_ref[flip, EDGE:, lanes]], axis=0)
                        )
                    acted[mask] = jnp.concatenate(near, axis=1)
                    continue
                place = others.index(mask)
                low = (2 * place + flip) * BLOCK
                near = []
                for tile in range(start // 128, stop // 128):
                    at = tile * 128 - start
                    spot = extended_ref.at[2 * place + flip, tile]
                    spot[:PAD] = halo[:, at : at + 128]
                    spot[PAD:] = mixed[low : low + BLOCK, at : at + 128]
                    half = filtered(spot, PAD, lanes_of(tile), taps, bias)
                    near.append(half_silu(half).astype(BF16))
                acted[mask] = jnp.concatenate(near, axis=1)
            if start == E:
                sides = []
                for mask in range(1, count):
                    maps = acted[mask].T[:N]
                    earlier = jnp.where((index ^ mask) < index, 1.0, 0.0).astype(BF16)
                    later = jnp.where((index ^ mask) < index, 0.0, 1.0).astype(BF16)
                    sides.append(jnp.concatenate([maps * earlier, maps * later], axis=0))
                writers[flip] = jnp.concatenate(sides, axis=1)
                continue
            fade = fades[flip]
            decayed = [
                fade[at * BLOCK : (at + 1) * BLOCK] * acted[at + 1]
                for at in range(count - 1)
            ]
            memory = dot(writers[flip], jnp.concatenate(decayed, axis=0))
            for way in range(2):
                kept = memory[way * N : (way + 1) * N]
                even = (iota(kept.shape, 1) & N) == 0
                chain = 2 * flip + way
                memory_ref[chain, :N, start:stop] = jnp.where(even, kept, 0.0).astype(BF16)
                memory_ref[chain, N:, start:stop] = jnp.where(even, 0.0, kept).astype(BF16)

    skip = wide_row(skip_gain_ref[...])
    for flip in range(2):
        for way in range(2):
            chain = 2 * flip + way
            spot = window_ref.at[chain]
            if way == 0:
                spot[PAD:] = edge_ref[flip, :EDGE]
            else:
                spot[:EDGE] = edge_ref[flip, EDGE:]
            at = PAD if way == 0 else 0
            half = filtered(spot, at, slice(0, MIXED), taps, bias, way == 1, EDGE)
            patch = half_silu(half).astype(BF16)

            def acted(tile):
                lanes = lanes_of(tile)
                if way == 0:
                    near = [patch[:, lanes], activated_ref[chain, EDGE:, lanes]]
                else:
                    near = [activated_ref[chain, : BLOCK - EDGE, lanes], patch[:, lanes]]
                return jnp.concatenate(near, axis=0)

            maps = acted(PAIRS)
            writer, reader = maps[:, :N], maps[:, N:]
            scores = jnp.where(lower if way == 0 else upper, dot_rows(reader, writer), 0.0)
            scores = scores.astype(BF16)
            squares = jnp.zeros((BLOCK, 128), F32)
            doubled = jnp.concatenate([reader, reader], axis=1)
            for pair in range(PAIRS):
                lanes = lanes_of(pair)
                signal = acted(pair)
                signals = jnp.concatenate(
                    [signal * left, signal * right, memory_ref[chain, :, lanes]], axis=0
                )
                weights = jnp.concatenate(
                    [
                        decay_ref[flip, 2 * pair + near] * scores
                        for near in range(2)
                    ]
                    + [lift_ref[chain, :, lanes] * doubled],
                    axis=1,
                )
                inside = dot(weights, signals)
                gated = inside + skip[:, lanes] * signal.astype(F32)
                gated = gated * silu_gate_ref[flip, :, lanes]
                squares = squares + gated * gated
                gated_ref[chain, :, lanes] = gated
            scale = lax.rsqrt(jnp.sum(squares, axis=1, keepdims=True) * (1.0 / E) + eps)
            for pair in range(PAIRS):
                lanes = lanes_of(pair)
                gated_ref[chain, :, lanes] = (
                    gated_ref[chain, :, lanes] * scale * gate_gain_ref[:, lanes]
                )

    normed = gated_ref[...].astype(BF16).reshape(4 * BLOCK, E)
    made = dot(normed, output_weight_ref[...])
    straight, crossed = made[: 2 * BLOCK], made[2 * BLOCK :]
    high, low = split(crossed, 2)
    both = straight + flip_lanes(high, swap) + flip_lanes(low, swap)
    backward = both[BLOCK:].astype(BF16).astype(F32)
    out_ref[...] = (both[:BLOCK] + backward).astype(BF16)


def wide_row(row):
    select = (iota((HEADS, E), 1) // N == iota((HEADS, E), 0)).astype(BF16)
    return exact_dot(jnp.broadcast_to(row, (8, HEADS)), select)[:1]


def swapped(rows, step, count):
    return lax.ppermute(rows, "seq", [(i, i ^ step) for i in range(count)])


def on_device(
    hidden,
    norm_gain,
    input_weight,
    step_weight,
    conv_weight,
    conv_bias,
    step_bias,
    log_rate,
    skip_gain,
    gate_gain,
    output_weight,
):
    count = lax.axis_size("seq")
    top = count // 2
    row = lambda vector: vector.reshape(1, -1)
    whole = pl.BlockSpec(memory_space=pltpu.VMEM)
    shape = jax.ShapeDtypeStruct
    gain, step_map = row(norm_gain), step_weight.T
    step_bias, log_rate = row(step_bias), row(log_rate)
    across = swapped(hidden, top, count)
    first = pl.pallas_call(
        lambda out_ref: out_ref.__setitem__(..., jnp.zeros((8, 128), F32)),
        out_shape=shape((8, 128), F32),
        out_specs=whole,
        compiler_params=pltpu.CompilerParams(vmem_limit_bytes=2**20),
        cost_estimate=pl.CostEstimate(flops=8 * 10**9, bytes_accessed=10**6, transcendentals=0),
        name="opening",
    )()

    def call(kernel, name, outs, scratch, operands, flops, limit, spec=whole):
        return pl.pallas_call(
            kernel,
            out_shape=outs,
            in_specs=[spec] * len(operands),
            out_specs=[whole] * len(outs),
            scratch_shapes=scratch,
            compiler_params=pltpu.CompilerParams(vmem_limit_bytes=limit * 2**20),
            cost_estimate=pl.CostEstimate(
                flops=flops, bytes_accessed=10**7, transcendentals=10**6
            ),
            name=name,
        )(*operands)

    operands = (
        hidden, gain, step_map, step_bias, log_rate, input_weight, conv_weight, conv_bias
    )
    decay, lift, *own = call(
        own_kernel,
        "own_rows",
        [
            shape((2, HEADS, BLOCK, BLOCK), BF16),
            shape((4, BLOCK, E), BF16),
            shape((4, BLOCK, MIXED), BF16),
            shape((2, 2 * EDGE, MIXED), F32),
            shape((2, BLOCK, E), F32),
        ],
        [pltpu.VMEM((2, TILES, BLOCK + 2 * PAD, 128), F32)],
        [first, *operands],
        2 * 10**9,
        16,
    )
    start, across, decay, lift, *own = lax.optimization_barrier(
        (hidden, across, decay, lift, *own)
    )
    received = {0: start, top: across}
    for bit in reversed(range(top.bit_length() - 1)):
        for mask in sorted(received):
            received[mask | 1 << bit] = swapped(received[mask], 1 << bit, count)
    shared = [gain, input_weight, step_map, conv_weight, conv_bias, step_bias, log_rate]
    ahead = call(
        functools.partial(ahead_kernel, top),
        "across_rows",
        [
            shape((2, BLOCK, MIXED), BF16),
            shape((2, EDGE + PAD, MIXED), F32),
            shape((HEADS, 2 * BLOCK), F32),
        ],
        [pltpu.VMEM((2, TILES, PAD + BLOCK, 128), F32)],
        [across, *shared],
        10**9,
        12,
    )
    others = [mask for mask in range(1, count) if mask != top]
    (out,) = call(
        functools.partial(join_kernel, count, top),
        "join_blocks",
        [shape((BLOCK, EMBED), BF16)],
        [
            pltpu.VMEM((2 * len(others) * BLOCK, EMBED), BF16),
            pltpu.VMEM((2 * len(others), TILES, PAD + BLOCK, 128), F32),
            pltpu.VMEM((4, 2 * N, E), BF16),
            pltpu.VMEM((4, PAD + EDGE, MIXED), F32),
            pltpu.VMEM((2, TILES, PAD + EDGE, 128), F32),
            pltpu.VMEM((4, BLOCK, E), F32),
        ],
        [
            *[received[mask] for mask in others],
            *shared,
            row(skip_gain),
            row(gate_gain),
            output_weight,
            decay,
            lift,
            *own,
            *ahead,
        ],
        2 * 10**9,
        18 + 2 * len(others),
    )
    return out


def solution(mesh):
    in_specs = (P(("batch", "seq"), None), P(), P(), P(), P(), P(), P(), P(), P(), P(), P())
    out_specs = P(("batch", "seq"), None)
    return jax.shard_map(
        on_device, mesh=mesh, in_specs=in_specs, out_specs=out_specs, check_vma=False
    )
```

```python
import functools

import jax
import jax.numpy as jnp
from jax import lax
from jax.experimental import pallas as pl
from jax.experimental.pallas import tpu as pltpu
from jax.sharding import PartitionSpec as P

EMBED = 512
E = 1024
N = 64
K = 4
BLOCK = 128
HEADS = 16
MIXED = E + 2 * N
TILES = MIXED // 128
PAIRS = E // 128
GROUPS = EMBED // 128
PAD = 8
EDGE = 16
UPFRONT = 4
eps = 1e-05
F32 = jnp.float32
BF16 = jnp.bfloat16


def dot(a, b):
    return jnp.dot(a, b, preferred_element_type=F32)


def dot_rows(a, b):
    return lax.dot_general(a, b, (((1,), (1,)), ((), ())), preferred_element_type=F32)


def iota(shape, axis):
    return lax.broadcasted_iota(jnp.int32, shape, axis)


def reversal():
    return (iota((128, 128), 0) + iota((128, 128), 1) == 127).astype(BF16)


def split(values, terms):
    parts = []
    for _ in range(terms):
        part = values.astype(BF16)
        parts.append(part)
        values = values - part.astype(F32)
    return parts


def exact_dot(values, mask):
    return sum(dot(part, mask) for part in split(values, 3))


def flip_lanes(rows, swap):
    return jnp.concatenate(
        [dot(rows[:, 128 * (GROUPS - 1 - g) : 128 * (GROUPS - g)], swap) for g in range(GROUPS)],
        axis=1,
    )


def both_normed(rows, gain, swap):
    floats = rows.astype(F32)
    scale = lax.rsqrt(jnp.mean(floats * floats, axis=-1, keepdims=True) + eps)
    flipped = flip_lanes(rows.astype(BF16), swap)
    return [(floats * scale * gain).astype(BF16), (flipped * scale * gain).astype(BF16)]


def half_silu(half):
    return half + half * jnp.tanh(half)


def column_of(row):
    shape = (HEADS, HEADS)
    return jnp.sum(
        jnp.where(iota(shape, 0) == iota(shape, 1), row, 0.0), axis=1, keepdims=True
    )


def log_decays(step_raw, step_bias, log_rate):
    v = step_raw + column_of(step_bias)
    u = jnp.exp(-jnp.abs(v))
    series = 1.0 / 7.0
    for order in range(6, 0, -1):
        series = 1.0 / order - u * series
    rest = jnp.where(u < 0.0625, u * series, jnp.log(1.0 + u))
    return -jnp.exp(column_of(log_rate)) * (jnp.maximum(v, 0.0) + rest)


def selectors(terms, heads):
    shape = (terms * HEADS, 256)
    head = iota(shape, 0) & (HEADS - 1)
    near = iota(shape, 1) >> (8 - (heads.bit_length() - 1))
    return [(head - near == low).astype(BF16) for low in range(0, HEADS, heads)]


def stacked_split(values, terms):
    return jnp.concatenate(split(values, terms), axis=0)


def dot_columns(a, b):
    return lax.dot_general(a, b, (((0,), (0,)), ((), ())), preferred_element_type=F32)


def lanes_of(tile):
    return slice(tile * 128, tile * 128 + 128)


def chunks(width):
    return [(start, min(start + 256, width)) for start in range(0, width, 256)]


def filtered(source, at, lanes, taps, bias, backward=False, rows=BLOCK):
    result = bias[:, lanes]
    for k in range(K):
        low = at + ((K - 1) - k if backward else k - (K - 1))
        result = result + taps[k : k + 1, lanes] * source[low : low + rows]
    return result


def own_kernel(
    opening_ref,
    x_ref,
    norm_gain_ref,
    step_weight_ref,
    step_bias_ref,
    log_rate_ref,
    input_weight_ref,
    conv_weight_ref,
    conv_bias_ref,
    decay_ref,
    lift_ref,
    activated_ref,
    edge_ref,
    silu_gate_ref,
    extended_ref,
):
    normal = jnp.concatenate(both_normed(x_ref[...], norm_gain_ref[...], reversal()), axis=0)
    log_decay = log_decays(
        dot_rows(step_weight_ref[...], normal), step_bias_ref[...], log_rate_ref[...]
    )
    row, column = iota((BLOCK, BLOCK), 0), iota((BLOCK, BLOCK), 1)
    lower = row >= column
    both = jnp.concatenate([log_decay[:, :BLOCK], log_decay[:, BLOCK:]], axis=0)
    before = exact_dot(both, (row <= column).astype(BF16))
    after = exact_dot(both, (row >= column).astype(BF16))
    twos, fours = selectors(3, 2), selectors(1, 4)
    ones = jnp.ones((3 * HEADS, BLOCK), BF16)

    def sides_of(rows):
        parts = stacked_split(rows, 3)
        return jnp.concatenate([parts, ones], axis=0), jnp.concatenate([-parts] * 2, axis=1)

    heads = [slice(flip * HEADS, (flip + 1) * HEADS) for flip in range(2)]
    sides = [[sides_of(rows[heads[flip]]) for rows in (before, after)] for flip in range(2)]
    lifts = [[jnp.exp(rows[heads[flip]]).astype(BF16) for rows in (before, after)] for flip in range(2)]

    def put_decay(flip, pair):
        spreads = [
            dot_columns(plus, jnp.concatenate([twos[pair], twos[pair] * minus], axis=0))
            for plus, minus in sides[flip]
        ]
        for near in range(2):
            lanes = lanes_of(near)
            decay_ref[flip, 2 * pair + near] = jnp.exp(
                jnp.where(lower, spreads[0][:, lanes], spreads[1][:, lanes])
            ).astype(BF16)

    def put_lift(flip, way, place):
        start, stop = chunks(E)[place]
        lift_ref[2 * flip + way, :, start:stop] = dot_columns(
            lifts[flip][way], fours[place]
        ).astype(BF16)

    spare = [functools.partial(put_decay, flip, pair) for flip in range(2) for pair in range(PAIRS)]
    spare += [
        functools.partial(put_lift, flip, way, place)
        for flip in range(2)
        for way in range(2)
        for place in range(PAIRS // 2)
    ]
    for _ in range(UPFRONT):
        spare.pop(0)()
    taps, bias = 0.5 * conv_weight_ref[...], 0.5 * conv_bias_ref[...].reshape(1, MIXED)
    for start, stop in chunks(MIXED):
        mixed = dot(normal, input_weight_ref[:, E + start : E + stop])
        for flip in range(2):
            rows = mixed[flip * BLOCK : (flip + 1) * BLOCK]
            edge_ref[flip, :EDGE, start:stop] = rows[:EDGE]
            edge_ref[flip, EDGE:, start:stop] = rows[BLOCK - EDGE :]
            for tile in range(start // 128, stop // 128):
                lanes = lanes_of(tile)
                place = extended_ref.at[flip, tile]
                place[:PAD] = jnp.zeros((PAD, 128), F32)
                place[PAD + BLOCK :] = jnp.zeros((PAD, 128), F32)
                place[PAD : PAD + BLOCK] = rows[:, tile * 128 - start : tile * 128 - start + 128]
        for flip in range(2):
            for tile in range(start // 128, stop // 128):
                lanes = lanes_of(tile)
                place = extended_ref.at[flip, tile]
                for way in range(2):
                    if spare:
                        spare.pop(0)()
                    half = filtered(place, PAD, lanes, taps, bias, way == 1)
                    activated_ref[2 * flip + way, :, lanes] = half_silu(half).astype(BF16)
    for start, stop in chunks(E):
        gate = dot(normal, input_weight_ref[:, start:stop])
        if spare:
            spare.pop(0)()
        gate = half_silu(0.5 * gate)
        for flip in range(2):
            silu_gate_ref[flip, :, start:stop] = gate[flip * BLOCK : (flip + 1) * BLOCK]
    for left_over in spare:
        left_over()


def chain_rows(mask, index, block, gain, swap):
    row, column = iota((BLOCK, BLOCK), 0), iota((BLOCK, BLOCK), 1)
    order = jnp.where((index ^ mask) < index, row, 127 - row) == column
    return both_normed(dot(order.astype(BF16), block), gain, swap)


def ahead_kernel(
    mask,
    block_ref,
    norm_gain_ref,
    input_weight_ref,
    step_weight_ref,
    conv_weight_ref,
    conv_bias_ref,
    step_bias_ref,
    log_rate_ref,
    activated_ref,
    edge_ref,
    log_decay_ref,
    extended_ref,
):
    index = lax.axis_index("seq")
    normal = jnp.concatenate(
        chain_rows(mask, index, block_ref[...], norm_gain_ref[...], reversal()), axis=0
    )
    log_decay_ref[...] = log_decays(
        dot_rows(step_weight_ref[...], normal), step_bias_ref[...], log_rate_ref[...]
    )
    taps, bias = 0.5 * conv_weight_ref[...], 0.5 * conv_bias_ref[...].reshape(1, MIXED)
    for start, stop in chunks(MIXED):
        mixed = dot(normal, input_weight_ref[:, E + start : E + stop])
        for flip in range(2):
            rows = mixed[flip * BLOCK : (flip + 1) * BLOCK]
            edge_ref[flip, :EDGE, start:stop] = rows[:EDGE]
            edge_ref[flip, EDGE:, start:stop] = rows[BLOCK - PAD :]
            for tile in range(start // 128, stop // 128):
                lanes = lanes_of(tile)
                place = extended_ref.at[flip, tile]
                place[:PAD] = jnp.zeros((PAD, 128), F32)
                place[PAD:] = rows[:, tile * 128 - start : tile * 128 - start + 128]
                half = filtered(place, PAD, lanes, taps, bias)
                activated_ref[flip, :, lanes] = half_silu(half).astype(BF16)


def join_kernel(count, early, *refs):
    others = [mask for mask in range(1, count) if mask not in early]
    received, refs = refs[: len(others)], refs[len(others) :]
    (
        norm_gain_ref,
        input_weight_ref,
        step_weight_ref,
        conv_weight_ref,
        conv_bias_ref,
        step_bias_ref,
        log_rate_ref,
        skip_gain_ref,
        gate_gain_ref,
        output_weight_ref,
        decay_ref,
        lift_ref,
        activated_ref,
        edge_ref,
        silu_gate_ref,
        *ahead_refs,
        out_ref,
        normal_ref,
        extended_ref,
        memory_ref,
        window_ref,
        patch_ref,
        gated_ref,
    ) = refs
    ahead = {mask: ahead_refs[3 * at : 3 * at + 3] for at, mask in enumerate(early)}
    index = lax.axis_index("seq")
    swap = reversal()
    row, column = iota((BLOCK, BLOCK), 0), iota((BLOCK, BLOCK), 1)
    lower, upper = row >= column, row <= column
    left, right = (column < N).astype(BF16), (column >= N).astype(BF16)
    taps, bias = 0.5 * conv_weight_ref[...], 0.5 * conv_bias_ref[...].reshape(1, MIXED)

    def picked(rows, block):
        result = jnp.zeros((PAD, rows[early[0]].shape[1]), F32)
        for mask, part in rows.items():
            result = jnp.where((index ^ mask) == block, part, result)
        return result

    for place, mask in enumerate(others):
        block = received[place][...]
        for flip, part in enumerate(chain_rows(mask, index, block, norm_gain_ref[...], swap)):
            low = (2 * place + flip) * BLOCK
            normal_ref[low : low + BLOCK] = part
    normal = normal_ref[...]
    log_decay = log_decays(
        dot_rows(step_weight_ref[...], normal), step_bias_ref[...], log_rate_ref[...]
    )
    pieces = {}
    for flip in range(2):
        for place, mask in enumerate(others):
            low = (2 * place + flip) * BLOCK
            pieces[mask, flip] = log_decay[:, low : low + BLOCK]
        for mask in early:
            pieces[mask, flip] = ahead[mask][2][:, flip * BLOCK : (flip + 1) * BLOCK]
    parts = [(mask, flip) for mask in range(1, count) for flip in range(2)]
    tails = exact_dot(
        jnp.concatenate([pieces[part] for part in parts], axis=0), (row > column).astype(BF16)
    )
    wholes = {part: jnp.sum(pieces[part], axis=1, keepdims=True) for part in parts}
    faded = [[], []]
    for at, (mask, flip) in enumerate(parts):
        tail = tails[at * HEADS : (at + 1) * HEADS]
        block = index ^ mask
        for other in range(1, count):
            if other != mask:
                between = index ^ other
                later = ((block < between) & (between < index)) | (
                    (index < between) & (between < block)
                )
                tail = tail + jnp.where(later, wholes[other, flip], 0.0)
        faded[flip].append(jnp.exp(tail))
    faded = [jnp.concatenate(rows, axis=1).astype(BF16) for rows in faded]
    fours = selectors(1, 4)

    writers = [None, None]
    order = chunks(MIXED)
    order = order[-1:] + order[:-1]

    def project(place):
        start, stop = order[place]
        return dot(normal, input_weight_ref[:, E + start : E + stop])

    def fade_of(place, flip):
        return dot_columns(faded[flip], fours[order[place][0] // 256]).astype(BF16)

    ready, coming = project(0), None
    for turn, (start, stop) in enumerate(order):
        mixed = ready
        if turn + 1 < len(order):
            ready = project(turn + 1)
            fades, coming = coming, [fade_of(turn + 1, flip) for flip in range(2)]
        else:
            fades = coming
        for flip in range(2):
            acted = {}
            last = {mask: ahead[mask][1][flip, EDGE:, start:stop] for mask in early}
            for place, mask in enumerate(others):
                low = (2 * place + flip) * BLOCK
                last[mask] = mixed[low + BLOCK - PAD : low + BLOCK]
            window_ref[2 * flip, :PAD, start:stop] = picked(last, index - 1)
            behind = picked(last, index + 1)
            for step in range(K - 1):
                spot = slice(EDGE + step, EDGE + step + 1)
                window_ref[2 * flip + 1, spot, start:stop] = behind[PAD - 1 - step : PAD - step]
            for mask in range(1, count):
                block = index ^ mask
                halo = picked(last, jnp.where(block < index, block - 1, block + 1))
                if mask in ahead:
                    near = []
                    ahead_ref, ahead_edge_ref, _ = ahead[mask]
                    for tile in range(start // 128, stop // 128):
                        lanes = lanes_of(tile)
                        spot = patch_ref.at[2 * early.index(mask) + flip, tile]
                        spot[:PAD] = halo[:, tile * 128 - start : tile * 128 - start + 128]
                        spot[PAD:] = ahead_edge_ref[flip, :EDGE, lanes]
                        half = filtered(spot, PAD, lanes, taps, bias, False, EDGE)
                        patch = half_silu(half).astype(BF16)
                        near.append(
                            jnp.concatenate([patch, ahead_ref[flip, EDGE:, lanes]], axis=0)
                        )
                    acted[mask] = jnp.concatenate(near, axis=1)
                    continue
                place = others.index(mask)
                low = (2 * place + flip) * BLOCK
                near = []
                for tile in range(start // 128, stop // 128):
                    at = tile * 128 - start
                    spot = extended_ref.at[2 * place + flip, tile]
                    spot[:PAD] = halo[:, at : at + 128]
                    spot[PAD:] = mixed[low : low + BLOCK, at : at + 128]
                    half = filtered(spot, PAD, lanes_of(tile), taps, bias)
                    near.append(half_silu(half).astype(BF16))
                acted[mask] = jnp.concatenate(near, axis=1)
            if start == E:
                sides = []
                for mask in range(1, count):
                    maps = acted[mask].T[:N]
                    earlier = jnp.where((index ^ mask) < index, 1.0, 0.0).astype(BF16)
                    later = jnp.where((index ^ mask) < index, 0.0, 1.0).astype(BF16)
                    sides.append(jnp.concatenate([maps * earlier, maps * later], axis=0))
                writers[flip] = jnp.concatenate(sides, axis=1)
                continue
            fade = fades[flip]
            decayed = [
                fade[at * BLOCK : (at + 1) * BLOCK] * acted[at + 1]
                for at in range(count - 1)
            ]
            memory = dot(writers[flip], jnp.concatenate(decayed, axis=0))
            for way in range(2):
                kept = memory[way * N : (way + 1) * N]
                even = (iota(kept.shape, 1) & N) == 0
                chain = 2 * flip + way
                memory_ref[chain, :N, start:stop] = jnp.where(even, kept, 0.0).astype(BF16)
                memory_ref[chain, N:, start:stop] = jnp.where(even, 0.0, kept).astype(BF16)

    skip = wide_row(skip_gain_ref[...])
    for flip in range(2):
        for way in range(2):
            chain = 2 * flip + way
            spot = window_ref.at[chain]
            if way == 0:
                spot[PAD:] = edge_ref[flip, :EDGE]
            else:
                spot[:EDGE] = edge_ref[flip, EDGE:]
            at = PAD if way == 0 else 0
            half = filtered(spot, at, slice(0, MIXED), taps, bias, way == 1, EDGE)
            patch = half_silu(half).astype(BF16)

            def acted(tile):
                lanes = lanes_of(tile)
                if way == 0:
                    near = [patch[:, lanes], activated_ref[chain, EDGE:, lanes]]
                else:
                    near = [activated_ref[chain, : BLOCK - EDGE, lanes], patch[:, lanes]]
                return jnp.concatenate(near, axis=0)

            maps = acted(PAIRS)
            writer, reader = maps[:, :N], maps[:, N:]
            scores = jnp.where(lower if way == 0 else upper, dot_rows(reader, writer), 0.0)
            scores = scores.astype(BF16)
            squares = jnp.zeros((BLOCK, 128), F32)
            doubled = jnp.concatenate([reader, reader], axis=1)
            for pair in range(PAIRS):
                lanes = lanes_of(pair)
                signal = acted(pair)
                signals = jnp.concatenate(
                    [signal * left, signal * right, memory_ref[chain, :, lanes]], axis=0
                )
                weights = jnp.concatenate(
                    [
                        decay_ref[flip, 2 * pair + near] * scores
                        for near in range(2)
                    ]
                    + [lift_ref[chain, :, lanes] * doubled],
                    axis=1,
                )
                inside = dot(weights, signals)
                gated = inside + skip[:, lanes] * signal.astype(F32)
                gated = gated * silu_gate_ref[flip, :, lanes]
                squares = squares + gated * gated
                gated_ref[chain, :, lanes] = gated
            scale = lax.rsqrt(jnp.sum(squares, axis=1, keepdims=True) * (1.0 / E) + eps)
            for pair in range(PAIRS):
                lanes = lanes_of(pair)
                gated_ref[chain, :, lanes] = (
                    gated_ref[chain, :, lanes] * scale * gate_gain_ref[:, lanes]
                )

    normed = gated_ref[...].astype(BF16).reshape(4 * BLOCK, E)
    made = dot(normed, output_weight_ref[...])
    straight, crossed = made[: 2 * BLOCK], made[2 * BLOCK :]
    high, low = split(crossed, 2)
    both = straight + flip_lanes(high, swap) + flip_lanes(low, swap)
    backward = both[BLOCK:].astype(BF16).astype(F32)
    out_ref[...] = (both[:BLOCK] + backward).astype(BF16)


def wide_row(row):
    select = (iota((HEADS, E), 1) // N == iota((HEADS, E), 0)).astype(BF16)
    return exact_dot(jnp.broadcast_to(row, (8, HEADS)), select)[:1]


def swapped(rows, step, count):
    return lax.ppermute(rows, "seq", [(i, i ^ step) for i in range(count)])


def on_device(
    hidden,
    norm_gain,
    input_weight,
    step_weight,
    conv_weight,
    conv_bias,
    step_bias,
    log_rate,
    skip_gain,
    gate_gain,
    output_weight,
):
    count = lax.axis_size("seq")
    top = count // 2
    row = lambda vector: vector.reshape(1, -1)
    whole = pl.BlockSpec(memory_space=pltpu.VMEM)
    shape = jax.ShapeDtypeStruct
    gain, step_map = row(norm_gain), step_weight.T
    step_bias, log_rate = row(step_bias), row(log_rate)
    across = swapped(hidden, top, count)
    first = pl.pallas_call(
        lambda out_ref: out_ref.__setitem__(..., jnp.zeros((8, 128), F32)),
        out_shape=shape((8, 128), F32),
        out_specs=whole,
        compiler_params=pltpu.CompilerParams(vmem_limit_bytes=2**20),
        cost_estimate=pl.CostEstimate(flops=8 * 10**9, bytes_accessed=10**6, transcendentals=0),
        name="opening",
    )()

    def call(kernel, name, outs, scratch, operands, flops, limit, spec=whole):
        return pl.pallas_call(
            kernel,
            out_shape=outs,
            in_specs=[spec] * len(operands),
            out_specs=[whole] * len(outs),
            scratch_shapes=scratch,
            compiler_params=pltpu.CompilerParams(vmem_limit_bytes=limit * 2**20),
            cost_estimate=pl.CostEstimate(
                flops=flops, bytes_accessed=10**7, transcendentals=10**6
            ),
            name=name,
        )(*operands)

    operands = (
        hidden, gain, step_map, step_bias, log_rate, input_weight, conv_weight, conv_bias
    )
    decay, lift, *own = call(
        own_kernel,
        "own_rows",
        [
            shape((2, HEADS, BLOCK, BLOCK), BF16),
            shape((4, BLOCK, E), BF16),
            shape((4, BLOCK, MIXED), BF16),
            shape((2, 2 * EDGE, MIXED), F32),
            shape((2, BLOCK, E), F32),
        ],
        [pltpu.VMEM((2, TILES, BLOCK + 2 * PAD, 128), F32)],
        [first, *operands],
        2 * 10**9,
        16,
    )
    shared = [gain, input_weight, step_map, conv_weight, conv_bias, step_bias, log_rate]

    def ahead(mask, block):
        return call(
            functools.partial(ahead_kernel, mask),
            "ahead_rows",
            [
                shape((2, BLOCK, MIXED), BF16),
                shape((2, EDGE + PAD, MIXED), F32),
                shape((HEADS, 2 * BLOCK), F32),
            ],
            [pltpu.VMEM((2, TILES, PAD + BLOCK, 128), F32)],
            [block, *shared],
            10**9,
            12,
        )

    done, received = {}, {0: hidden}
    if top > 1:
        received[1] = swapped(hidden, 1, count)
        done[1] = ahead(1, received[1])
    across, decay, lift, own, done = lax.optimization_barrier((across, decay, lift, own, done))
    received[top] = across
    for bit in reversed(range(top.bit_length() - 1)):
        for mask in sorted(received):
            if not mask & ((2 << bit) - 1) and mask | 1 << bit not in received:
                received[mask | 1 << bit] = swapped(received[mask], 1 << bit, count)
    done[top] = ahead(top, across)
    others = [mask for mask in range(1, count) if mask not in done]
    (out,) = call(
        functools.partial(join_kernel, count, sorted(done)),
        "join_blocks",
        [shape((BLOCK, EMBED), BF16)],
        [
            pltpu.VMEM((2 * len(others) * BLOCK, EMBED), BF16),
            pltpu.VMEM((2 * len(others), TILES, PAD + BLOCK, 128), F32),
            pltpu.VMEM((4, 2 * N, E), BF16),
            pltpu.VMEM((4, PAD + EDGE, MIXED), F32),
            pltpu.VMEM((2 * len(done), TILES, PAD + EDGE, 128), F32),
            pltpu.VMEM((4, BLOCK, E), F32),
        ],
        [
            *[received[mask] for mask in others],
            *shared,
            row(skip_gain),
            row(gate_gain),
            output_weight,
            decay,
            lift,
            *own,
            *[part for mask in sorted(done) for part in done[mask]],
        ],
        2 * 10**9,
        18 + 2 * len(others),
    )
    return out


def solution(mesh):
    in_specs = (P(("batch", "seq"), None), P(), P(), P(), P(), P(), P(), P(), P(), P(), P())
    out_specs = P(("batch", "seq"), None)
    return jax.shard_map(
        on_device, mesh=mesh, in_specs=in_specs, out_specs=out_specs, check_vma=False
    )
```

```python
import functools

import jax
import jax.numpy as jnp
from jax import lax
from jax.experimental import pallas as pl
from jax.experimental.pallas import tpu as pltpu
from jax.sharding import PartitionSpec as P

EMBED = 512
E = 1024
N = 64
K = 4
BLOCK = 128
HEADS = 16
MIXED = E + 2 * N
TILES = MIXED // 128
PAIRS = E // 128
GROUPS = EMBED // 128
PAD = 8
EDGE = 16
UPFRONT = 0
eps = 1e-05
F32 = jnp.float32
BF16 = jnp.bfloat16


def dot(a, b):
    return jnp.dot(a, b, preferred_element_type=F32)


def dot_rows(a, b):
    return lax.dot_general(a, b, (((1,), (1,)), ((), ())), preferred_element_type=F32)


def iota(shape, axis):
    return lax.broadcasted_iota(jnp.int32, shape, axis)


def reversal():
    return (iota((128, 128), 0) + iota((128, 128), 1) == 127).astype(BF16)


def split(values, terms):
    parts = []
    for _ in range(terms):
        part = values.astype(BF16)
        parts.append(part)
        values = values - part.astype(F32)
    return parts


def exact_dot(values, mask):
    return sum(dot(part, mask) for part in split(values, 3))


def flip_lanes(rows, swap):
    return jnp.concatenate(
        [dot(rows[:, 128 * (GROUPS - 1 - g) : 128 * (GROUPS - g)], swap) for g in range(GROUPS)],
        axis=1,
    )


def both_normed(rows, gain, swap):
    floats = rows.astype(F32)
    scale = lax.rsqrt(jnp.mean(floats * floats, axis=-1, keepdims=True) + eps)
    flipped = flip_lanes(rows.astype(BF16), swap)
    return [(floats * scale * gain).astype(BF16), (flipped * scale * gain).astype(BF16)]


def half_silu(half):
    return half + half * jnp.tanh(half)


def column_of(row):
    shape = (HEADS, HEADS)
    return jnp.sum(
        jnp.where(iota(shape, 0) == iota(shape, 1), row, 0.0), axis=1, keepdims=True
    )


def log_decays(step_raw, step_bias, log_rate):
    v = step_raw + column_of(step_bias)
    u = jnp.exp(-jnp.abs(v))
    series = 1.0 / 7.0
    for order in range(6, 0, -1):
        series = 1.0 / order - u * series
    rest = jnp.where(u < 0.0625, u * series, jnp.log(1.0 + u))
    return -jnp.exp(column_of(log_rate)) * (jnp.maximum(v, 0.0) + rest)


def selectors(terms, heads):
    shape = (terms * HEADS, 256)
    head = iota(shape, 0) & (HEADS - 1)
    near = iota(shape, 1) >> (8 - (heads.bit_length() - 1))
    return [(head - near == low).astype(BF16) for low in range(0, HEADS, heads)]


def stacked_split(values, terms):
    return jnp.concatenate(split(values, terms), axis=0)


def dot_columns(a, b):
    return lax.dot_general(a, b, (((0,), (0,)), ((), ())), preferred_element_type=F32)


def lanes_of(tile):
    return slice(tile * 128, tile * 128 + 128)


def chunks(width):
    return [(start, min(start + 256, width)) for start in range(0, width, 256)]


def filtered(source, at, lanes, taps, bias, backward=False, rows=BLOCK):
    result = bias[:, lanes]
    for k in range(K):
        low = at + ((K - 1) - k if backward else k - (K - 1))
        result = result + taps[k : k + 1, lanes] * source[low : low + rows]
    return result


def own_kernel(
    opening_ref,
    x_ref,
    norm_gain_ref,
    step_weight_ref,
    step_bias_ref,
    log_rate_ref,
    input_weight_ref,
    conv_weight_ref,
    conv_bias_ref,
    decay_ref,
    lift_ref,
    activated_ref,
    edge_ref,
    silu_gate_ref,
    extended_ref,
):
    normal = jnp.concatenate(both_normed(x_ref[...], norm_gain_ref[...], reversal()), axis=0)
    log_decay = log_decays(
        dot_rows(step_weight_ref[...], normal), step_bias_ref[...], log_rate_ref[...]
    )
    row, column = iota((BLOCK, BLOCK), 0), iota((BLOCK, BLOCK), 1)
    lower = row >= column
    both = jnp.concatenate([log_decay[:, :BLOCK], log_decay[:, BLOCK:]], axis=0)
    before = exact_dot(both, (row <= column).astype(BF16))
    after = exact_dot(both, (row >= column).astype(BF16))
    twos, fours = selectors(3, 2), selectors(1, 4)
    ones = jnp.ones((3 * HEADS, BLOCK), BF16)

    def sides_of(rows):
        parts = stacked_split(rows, 3)
        return jnp.concatenate([parts, ones], axis=0), jnp.concatenate([-parts] * 2, axis=1)

    heads = [slice(flip * HEADS, (flip + 1) * HEADS) for flip in range(2)]
    sides = [[sides_of(rows[heads[flip]]) for rows in (before, after)] for flip in range(2)]
    lifts = [[jnp.exp(rows[heads[flip]]).astype(BF16) for rows in (before, after)] for flip in range(2)]

    def put_decay(flip, pair):
        spreads = [
            dot_columns(plus, jnp.concatenate([twos[pair], twos[pair] * minus], axis=0))
            for plus, minus in sides[flip]
        ]
        for near in range(2):
            lanes = lanes_of(near)
            decay_ref[flip, 2 * pair + near] = jnp.exp(
                jnp.where(lower, spreads[0][:, lanes], spreads[1][:, lanes])
            ).astype(BF16)

    def put_lift(flip, way, place):
        start, stop = chunks(E)[place]
        lift_ref[2 * flip + way, :, start:stop] = dot_columns(
            lifts[flip][way], fours[place]
        ).astype(BF16)

    spare = [functools.partial(put_decay, flip, pair) for flip in range(2) for pair in range(PAIRS)]
    spare += [
        functools.partial(put_lift, flip, way, place)
        for flip in range(2)
        for way in range(2)
        for place in range(PAIRS // 2)
    ]
    for _ in range(UPFRONT):
        spare.pop(0)()
    taps, bias = 0.5 * conv_weight_ref[...], 0.5 * conv_bias_ref[...].reshape(1, MIXED)
    order = chunks(MIXED)
    ready = dot(normal, input_weight_ref[:, E : E + order[0][1]])
    for turn, (start, stop) in enumerate(order):
        mixed = ready
        if turn + 1 < len(order):
            ready = dot(normal, input_weight_ref[:, E + stop : E + order[turn + 1][1]])
        for flip in range(2):
            rows = mixed[flip * BLOCK : (flip + 1) * BLOCK]
            edge_ref[flip, :EDGE, start:stop] = rows[:EDGE]
            edge_ref[flip, EDGE:, start:stop] = rows[BLOCK - EDGE :]
            for tile in range(start // 128, stop // 128):
                lanes = lanes_of(tile)
                place = extended_ref.at[flip, tile]
                place[:PAD] = jnp.zeros((PAD, 128), F32)
                place[PAD + BLOCK :] = jnp.zeros((PAD, 128), F32)
                place[PAD : PAD + BLOCK] = rows[:, tile * 128 - start : tile * 128 - start + 128]
        for flip in range(2):
            for tile in range(start // 128, stop // 128):
                lanes = lanes_of(tile)
                place = extended_ref.at[flip, tile]
                for way in range(2):
                    if spare:
                        spare.pop(0)()
                    half = filtered(place, PAD, lanes, taps, bias, way == 1)
                    activated_ref[2 * flip + way, :, lanes] = half_silu(half).astype(BF16)
    for start, stop in chunks(E):
        gate = dot(normal, input_weight_ref[:, start:stop])
        if spare:
            spare.pop(0)()
        gate = half_silu(0.5 * gate)
        for flip in range(2):
            silu_gate_ref[flip, :, start:stop] = gate[flip * BLOCK : (flip + 1) * BLOCK]
    for left_over in spare:
        left_over()


def chain_rows(mask, index, block, gain, swap):
    row, column = iota((BLOCK, BLOCK), 0), iota((BLOCK, BLOCK), 1)
    order = jnp.where((index ^ mask) < index, row, 127 - row) == column
    return both_normed(dot(order.astype(BF16), block), gain, swap)


def ahead_kernel(
    mask,
    block_ref,
    norm_gain_ref,
    input_weight_ref,
    step_weight_ref,
    conv_weight_ref,
    conv_bias_ref,
    step_bias_ref,
    log_rate_ref,
    activated_ref,
    edge_ref,
    log_decay_ref,
    extended_ref,
):
    index = lax.axis_index("seq")
    normal = jnp.concatenate(
        chain_rows(mask, index, block_ref[...], norm_gain_ref[...], reversal()), axis=0
    )
    log_decay_ref[...] = log_decays(
        dot_rows(step_weight_ref[...], normal), step_bias_ref[...], log_rate_ref[...]
    )
    taps, bias = 0.5 * conv_weight_ref[...], 0.5 * conv_bias_ref[...].reshape(1, MIXED)
    order = chunks(MIXED)
    ready = dot(normal, input_weight_ref[:, E : E + order[0][1]])
    for turn, (start, stop) in enumerate(order):
        mixed = ready
        if turn + 1 < len(order):
            ready = dot(normal, input_weight_ref[:, E + stop : E + order[turn + 1][1]])
        for flip in range(2):
            rows = mixed[flip * BLOCK : (flip + 1) * BLOCK]
            edge_ref[flip, :EDGE, start:stop] = rows[:EDGE]
            edge_ref[flip, EDGE:, start:stop] = rows[BLOCK - PAD :]
            for tile in range(start // 128, stop // 128):
                lanes = lanes_of(tile)
                place = extended_ref.at[flip, tile]
                place[:PAD] = jnp.zeros((PAD, 128), F32)
                place[PAD:] = rows[:, tile * 128 - start : tile * 128 - start + 128]
                half = filtered(place, PAD, lanes, taps, bias)
                activated_ref[flip, :, lanes] = half_silu(half).astype(BF16)


def join_kernel(count, early, *refs):
    others = [mask for mask in range(1, count) if mask not in early]
    received, refs = refs[: len(others)], refs[len(others) :]
    (
        norm_gain_ref,
        input_weight_ref,
        step_weight_ref,
        conv_weight_ref,
        conv_bias_ref,
        step_bias_ref,
        log_rate_ref,
        skip_gain_ref,
        gate_gain_ref,
        output_weight_ref,
        decay_ref,
        lift_ref,
        activated_ref,
        edge_ref,
        silu_gate_ref,
        *ahead_refs,
        out_ref,
        normal_ref,
        extended_ref,
        memory_ref,
        window_ref,
        patch_ref,
        gated_ref,
    ) = refs
    ahead = {mask: ahead_refs[3 * at : 3 * at + 3] for at, mask in enumerate(early)}
    index = lax.axis_index("seq")
    swap = reversal()
    row, column = iota((BLOCK, BLOCK), 0), iota((BLOCK, BLOCK), 1)
    lower, upper = row >= column, row <= column
    left, right = (column < N).astype(BF16), (column >= N).astype(BF16)
    taps, bias = 0.5 * conv_weight_ref[...], 0.5 * conv_bias_ref[...].reshape(1, MIXED)

    def picked(rows, block):
        result = jnp.zeros((PAD, rows[early[0]].shape[1]), F32)
        for mask, part in rows.items():
            result = jnp.where((index ^ mask) == block, part, result)
        return result

    for place, mask in enumerate(others):
        block = received[place][...]
        for flip, part in enumerate(chain_rows(mask, index, block, norm_gain_ref[...], swap)):
            low = (2 * place + flip) * BLOCK
            normal_ref[low : low + BLOCK] = part
    normal = normal_ref[...]
    log_decay = log_decays(
        dot_rows(step_weight_ref[...], normal), step_bias_ref[...], log_rate_ref[...]
    )
    pieces = {}
    for flip in range(2):
        for place, mask in enumerate(others):
            low = (2 * place + flip) * BLOCK
            pieces[mask, flip] = log_decay[:, low : low + BLOCK]
        for mask in early:
            pieces[mask, flip] = ahead[mask][2][:, flip * BLOCK : (flip + 1) * BLOCK]
    parts = [(mask, flip) for mask in range(1, count) for flip in range(2)]
    tails = exact_dot(
        jnp.concatenate([pieces[part] for part in parts], axis=0), (row > column).astype(BF16)
    )
    wholes = {part: jnp.sum(pieces[part], axis=1, keepdims=True) for part in parts}
    faded = [[], []]
    for at, (mask, flip) in enumerate(parts):
        tail = tails[at * HEADS : (at + 1) * HEADS]
        block = index ^ mask
        for other in range(1, count):
            if other != mask:
                between = index ^ other
                later = ((block < between) & (between < index)) | (
                    (index < between) & (between < block)
                )
                tail = tail + jnp.where(later, wholes[other, flip], 0.0)
        faded[flip].append(jnp.exp(tail))
    faded = [jnp.concatenate(rows, axis=1).astype(BF16) for rows in faded]
    fours = selectors(1, 4)

    writers = [None, None]
    order = chunks(MIXED)
    order = order[-1:] + order[:-1]

    def project(place):
        start, stop = order[place]
        return dot(normal, input_weight_ref[:, E + start : E + stop])

    def fade_of(place, flip):
        return dot_columns(faded[flip], fours[order[place][0] // 256]).astype(BF16)

    ready, coming = project(0), None
    for turn, (start, stop) in enumerate(order):
        mixed = ready
        if turn + 1 < len(order):
            ready = project(turn + 1)
            fades, coming = coming, [fade_of(turn + 1, flip) for flip in range(2)]
        else:
            fades = coming
        for flip in range(2):
            acted = {}
            last = {mask: ahead[mask][1][flip, EDGE:, start:stop] for mask in early}
            for place, mask in enumerate(others):
                low = (2 * place + flip) * BLOCK
                last[mask] = mixed[low + BLOCK - PAD : low + BLOCK]
            window_ref[2 * flip, :PAD, start:stop] = picked(last, index - 1)
            behind = picked(last, index + 1)
            for step in range(K - 1):
                spot = slice(EDGE + step, EDGE + step + 1)
                window_ref[2 * flip + 1, spot, start:stop] = behind[PAD - 1 - step : PAD - step]
            for mask in range(1, count):
                block = index ^ mask
                halo = picked(last, jnp.where(block < index, block - 1, block + 1))
                if mask in ahead:
                    near = []
                    ahead_ref, ahead_edge_ref, _ = ahead[mask]
                    for tile in range(start // 128, stop // 128):
                        lanes = lanes_of(tile)
                        spot = patch_ref.at[2 * early.index(mask) + flip, tile]
                        spot[:PAD] = halo[:, tile * 128 - start : tile * 128 - start + 128]
                        spot[PAD:] = ahead_edge_ref[flip, :EDGE, lanes]
                        half = filtered(spot, PAD, lanes, taps, bias, False, EDGE)
                        patch = half_silu(half).astype(BF16)
                        near.append(
                            jnp.concatenate([patch, ahead_ref[flip, EDGE:, lanes]], axis=0)
                        )
                    acted[mask] = jnp.concatenate(near, axis=1)
                    continue
                place = others.index(mask)
                low = (2 * place + flip) * BLOCK
                near = []
                for tile in range(start // 128, stop // 128):
                    at = tile * 128 - start
                    spot = extended_ref.at[2 * place + flip, tile]
                    spot[:PAD] = halo[:, at : at + 128]
                    spot[PAD:] = mixed[low : low + BLOCK, at : at + 128]
                    half = filtered(spot, PAD, lanes_of(tile), taps, bias)
                    near.append(half_silu(half).astype(BF16))
                acted[mask] = jnp.concatenate(near, axis=1)
            if start == E:
                sides = []
                for mask in range(1, count):
                    maps = acted[mask].T[:N]
                    earlier = jnp.where((index ^ mask) < index, 1.0, 0.0).astype(BF16)
                    later = jnp.where((index ^ mask) < index, 0.0, 1.0).astype(BF16)
                    sides.append(jnp.concatenate([maps * earlier, maps * later], axis=0))
                writers[flip] = jnp.concatenate(sides, axis=1)
                continue
            fade = fades[flip]
            decayed = [
                fade[at * BLOCK : (at + 1) * BLOCK] * acted[at + 1]
                for at in range(count - 1)
            ]
            memory = dot(writers[flip], jnp.concatenate(decayed, axis=0))
            for way in range(2):
                kept = memory[way * N : (way + 1) * N]
                even = (iota(kept.shape, 1) & N) == 0
                chain = 2 * flip + way
                memory_ref[chain, :N, start:stop] = jnp.where(even, kept, 0.0).astype(BF16)
                memory_ref[chain, N:, start:stop] = jnp.where(even, 0.0, kept).astype(BF16)

    skip = wide_row(skip_gain_ref[...])
    for flip in range(2):
        for way in range(2):
            chain = 2 * flip + way
            spot = window_ref.at[chain]
            if way == 0:
                spot[PAD:] = edge_ref[flip, :EDGE]
            else:
                spot[:EDGE] = edge_ref[flip, EDGE:]
            at = PAD if way == 0 else 0
            half = filtered(spot, at, slice(0, MIXED), taps, bias, way == 1, EDGE)
            patch = half_silu(half).astype(BF16)

            def acted(tile):
                lanes = lanes_of(tile)
                if way == 0:
                    near = [patch[:, lanes], activated_ref[chain, EDGE:, lanes]]
                else:
                    near = [activated_ref[chain, : BLOCK - EDGE, lanes], patch[:, lanes]]
                return jnp.concatenate(near, axis=0)

            maps = acted(PAIRS)
            writer, reader = maps[:, :N], maps[:, N:]
            scores = jnp.where(lower if way == 0 else upper, dot_rows(reader, writer), 0.0)
            scores = scores.astype(BF16)
            squares = jnp.zeros((BLOCK, 128), F32)
            doubled = jnp.concatenate([reader, reader], axis=1)
            for pair in range(PAIRS):
                lanes = lanes_of(pair)
                signal = acted(pair)
                signals = jnp.concatenate(
                    [signal * left, signal * right, memory_ref[chain, :, lanes]], axis=0
                )
                weights = jnp.concatenate(
                    [
                        decay_ref[flip, 2 * pair + near] * scores
                        for near in range(2)
                    ]
                    + [lift_ref[chain, :, lanes] * doubled],
                    axis=1,
                )
                inside = dot(weights, signals)
                gated = inside + skip[:, lanes] * signal.astype(F32)
                gated = gated * silu_gate_ref[flip, :, lanes]
                squares = squares + gated * gated
                gated_ref[chain, :, lanes] = gated
            scale = lax.rsqrt(jnp.sum(squares, axis=1, keepdims=True) * (1.0 / E) + eps)
            for pair in range(PAIRS):
                lanes = lanes_of(pair)
                gated_ref[chain, :, lanes] = (
                    gated_ref[chain, :, lanes] * scale * gate_gain_ref[:, lanes]
                )

    normed = gated_ref[...].astype(BF16).reshape(4 * BLOCK, E)
    made = dot(normed, output_weight_ref[...])
    straight, crossed = made[: 2 * BLOCK], made[2 * BLOCK :]
    high, low = split(crossed, 2)
    both = straight + flip_lanes(high, swap) + flip_lanes(low, swap)
    backward = both[BLOCK:].astype(BF16).astype(F32)
    out_ref[...] = (both[:BLOCK] + backward).astype(BF16)


def wide_row(row):
    select = (iota((HEADS, E), 1) // N == iota((HEADS, E), 0)).astype(BF16)
    return exact_dot(jnp.broadcast_to(row, (8, HEADS)), select)[:1]


def swapped(rows, step, count):
    return lax.ppermute(rows, "seq", [(i, i ^ step) for i in range(count)])


def on_device(
    hidden,
    norm_gain,
    input_weight,
    step_weight,
    conv_weight,
    conv_bias,
    step_bias,
    log_rate,
    skip_gain,
    gate_gain,
    output_weight,
):
    count = lax.axis_size("seq")
    top = count // 2
    row = lambda vector: vector.reshape(1, -1)
    whole = pl.BlockSpec(memory_space=pltpu.VMEM)
    shape = jax.ShapeDtypeStruct
    gain, step_map = row(norm_gain), step_weight.T
    step_bias, log_rate = row(step_bias), row(log_rate)
    across = swapped(hidden, top, count)
    first = pl.pallas_call(
        lambda out_ref: out_ref.__setitem__(..., jnp.zeros((8, 128), F32)),
        out_shape=shape((8, 128), F32),
        out_specs=whole,
        compiler_params=pltpu.CompilerParams(vmem_limit_bytes=2**20),
        cost_estimate=pl.CostEstimate(flops=8 * 10**9, bytes_accessed=10**6, transcendentals=0),
        name="opening",
    )()

    def call(kernel, name, outs, scratch, operands, flops, limit, spec=whole):
        return pl.pallas_call(
            kernel,
            out_shape=outs,
            in_specs=[spec] * len(operands),
            out_specs=[whole] * len(outs),
            scratch_shapes=scratch,
            compiler_params=pltpu.CompilerParams(vmem_limit_bytes=limit * 2**20),
            cost_estimate=pl.CostEstimate(
                flops=flops, bytes_accessed=10**7, transcendentals=10**6
            ),
            name=name,
        )(*operands)

    operands = (
        hidden, gain, step_map, step_bias, log_rate, input_weight, conv_weight, conv_bias
    )
    decay, lift, *own = call(
        own_kernel,
        "own_rows",
        [
            shape((2, HEADS, BLOCK, BLOCK), BF16),
            shape((4, BLOCK, E), BF16),
            shape((4, BLOCK, MIXED), BF16),
            shape((2, 2 * EDGE, MIXED), F32),
            shape((2, BLOCK, E), F32),
        ],
        [pltpu.VMEM((2, TILES, BLOCK + 2 * PAD, 128), F32)],
        [first, *operands],
        2 * 10**9,
        16,
    )
    shared = [gain, input_weight, step_map, conv_weight, conv_bias, step_bias, log_rate]

    def ahead(mask, block):
        return call(
            functools.partial(ahead_kernel, mask),
            "ahead_rows",
            [
                shape((2, BLOCK, MIXED), BF16),
                shape((2, EDGE + PAD, MIXED), F32),
                shape((HEADS, 2 * BLOCK), F32),
            ],
            [pltpu.VMEM((2, TILES, PAD + BLOCK, 128), F32)],
            [block, *shared],
            10**9,
            12,
        )

    done, received = {}, {0: hidden}
    if top > 1:
        received[1] = swapped(hidden, 1, count)
        done[1] = ahead(1, received[1])
    across, decay, lift, own, done = lax.optimization_barrier((across, decay, lift, own, done))
    received[top] = across
    for bit in reversed(range(top.bit_length() - 1)):
        for mask in sorted(received):
            if not mask & ((2 << bit) - 1) and mask | 1 << bit not in received:
                received[mask | 1 << bit] = swapped(received[mask], 1 << bit, count)
    done[top] = ahead(top, across)
    others = [mask for mask in range(1, count) if mask not in done]
    (out,) = call(
        functools.partial(join_kernel, count, sorted(done)),
        "join_blocks",
        [shape((BLOCK, EMBED), BF16)],
        [
            pltpu.VMEM((2 * len(others) * BLOCK, EMBED), BF16),
            pltpu.VMEM((2 * len(others), TILES, PAD + BLOCK, 128), F32),
            pltpu.VMEM((4, 2 * N, E), BF16),
            pltpu.VMEM((4, PAD + EDGE, MIXED), F32),
            pltpu.VMEM((2 * len(done), TILES, PAD + EDGE, 128), F32),
            pltpu.VMEM((4, BLOCK, E), F32),
        ],
        [
            *[received[mask] for mask in others],
            *shared,
            row(skip_gain),
            row(gate_gain),
            output_weight,
            decay,
            lift,
            *own,
            *[part for mask in sorted(done) for part in done[mask]],
        ],
        2 * 10**9,
        18 + 2 * len(others),
    )
    return out


def solution(mesh):
    in_specs = (P(("batch", "seq"), None), P(), P(), P(), P(), P(), P(), P(), P(), P(), P())
    out_specs = P(("batch", "seq"), None)
    return jax.shard_map(
        on_device, mesh=mesh, in_specs=in_specs, out_specs=out_specs, check_vma=False
    )
```

```python
import functools

import jax
import jax.numpy as jnp
from jax import lax
from jax.experimental import pallas as pl
from jax.experimental.pallas import tpu as pltpu
from jax.sharding import PartitionSpec as P

EMBED = 512
E = 1024
N = 64
K = 4
BLOCK = 128
HEADS = 16
MIXED = E + 2 * N
TILES = MIXED // 128
PAIRS = E // 128
GROUPS = EMBED // 128
PAD = 8
EDGE = 16
UPFRONT = 0
eps = 1e-05
F32 = jnp.float32
BF16 = jnp.bfloat16


def dot(a, b):
    return jnp.dot(a, b, preferred_element_type=F32)


def dot_rows(a, b):
    return lax.dot_general(a, b, (((1,), (1,)), ((), ())), preferred_element_type=F32)


def iota(shape, axis):
    return lax.broadcasted_iota(jnp.int32, shape, axis)


def reversal():
    return (iota((128, 128), 0) + iota((128, 128), 1) == 127).astype(BF16)


def split(values, terms):
    parts = []
    for _ in range(terms):
        part = values.astype(BF16)
        parts.append(part)
        values = values - part.astype(F32)
    return parts


def exact_dot(values, mask):
    return sum(dot(part, mask) for part in split(values, 3))


def flip_lanes(rows, swap):
    return jnp.concatenate(
        [dot(rows[:, 128 * (GROUPS - 1 - g) : 128 * (GROUPS - g)], swap) for g in range(GROUPS)],
        axis=1,
    )


def both_normed(rows, gain, swap):
    floats = rows.astype(F32)
    scale = lax.rsqrt(jnp.mean(floats * floats, axis=-1, keepdims=True) + eps)
    flipped = flip_lanes(rows.astype(BF16), swap)
    return [(floats * scale * gain).astype(BF16), (flipped * scale * gain).astype(BF16)]


def half_silu(half):
    return half + half * jnp.tanh(half)


def column_of(row):
    shape = (HEADS, HEADS)
    return jnp.sum(
        jnp.where(iota(shape, 0) == iota(shape, 1), row, 0.0), axis=1, keepdims=True
    )


def log_decays(step_raw, step_bias, log_rate):
    v = step_raw + column_of(step_bias)
    u = jnp.exp(-jnp.abs(v))
    series = 1.0 / 7.0
    for order in range(6, 0, -1):
        series = 1.0 / order - u * series
    rest = jnp.where(u < 0.0625, u * series, jnp.log(1.0 + u))
    return -jnp.exp(column_of(log_rate)) * (jnp.maximum(v, 0.0) + rest)


def selectors(terms, heads):
    shape = (terms * HEADS, 256)
    head = iota(shape, 0) & (HEADS - 1)
    near = iota(shape, 1) >> (8 - (heads.bit_length() - 1))
    return [(head - near == low).astype(BF16) for low in range(0, HEADS, heads)]


def stacked_split(values, terms):
    return jnp.concatenate(split(values, terms), axis=0)


def dot_columns(a, b):
    return lax.dot_general(a, b, (((0,), (0,)), ((), ())), preferred_element_type=F32)


def lanes_of(tile):
    return slice(tile * 128, tile * 128 + 128)


def chunks(width):
    return [(start, min(start + 256, width)) for start in range(0, width, 256)]


def filtered(source, at, lanes, taps, bias, backward=False, rows=BLOCK):
    result = bias[:, lanes]
    for k in range(K):
        low = at + ((K - 1) - k if backward else k - (K - 1))
        result = result + taps[k : k + 1, lanes] * source[low : low + rows]
    return result


def own_kernel(
    opening_ref,
    x_ref,
    norm_gain_ref,
    step_weight_ref,
    step_bias_ref,
    log_rate_ref,
    input_weight_ref,
    conv_weight_ref,
    conv_bias_ref,
    decay_ref,
    lift_ref,
    activated_ref,
    edge_ref,
    silu_gate_ref,
    extended_ref,
):
    normal = jnp.concatenate(both_normed(x_ref[...], norm_gain_ref[...], reversal()), axis=0)
    log_decay = log_decays(
        dot_rows(step_weight_ref[...], normal), step_bias_ref[...], log_rate_ref[...]
    )
    row, column = iota((BLOCK, BLOCK), 0), iota((BLOCK, BLOCK), 1)
    lower = row >= column
    both = jnp.concatenate([log_decay[:, :BLOCK], log_decay[:, BLOCK:]], axis=0)
    before = exact_dot(both, (row <= column).astype(BF16))
    after = exact_dot(both, (row >= column).astype(BF16))
    twos, fours = selectors(3, 2), selectors(1, 4)
    ones = jnp.ones((3 * HEADS, BLOCK), BF16)

    def sides_of(rows):
        parts = stacked_split(rows, 3)
        return jnp.concatenate([parts, ones], axis=0), jnp.concatenate([-parts] * 2, axis=1)

    heads = [slice(flip * HEADS, (flip + 1) * HEADS) for flip in range(2)]
    sides = [[sides_of(rows[heads[flip]]) for rows in (before, after)] for flip in range(2)]
    lifts = [[jnp.exp(rows[heads[flip]]).astype(BF16) for rows in (before, after)] for flip in range(2)]

    def put_decay(flip, pair):
        spreads = [
            dot_columns(plus, jnp.concatenate([twos[pair], twos[pair] * minus], axis=0))
            for plus, minus in sides[flip]
        ]
        for near in range(2):
            lanes = lanes_of(near)
            decay_ref[flip, 2 * pair + near] = jnp.exp(
                jnp.where(lower, spreads[0][:, lanes], spreads[1][:, lanes])
            ).astype(BF16)

    def put_lift(flip, way, place):
        start, stop = chunks(E)[place]
        lift_ref[2 * flip + way, :, start:stop] = dot_columns(
            lifts[flip][way], fours[place]
        ).astype(BF16)

    spare = [functools.partial(put_decay, flip, pair) for flip in range(2) for pair in range(PAIRS)]
    spare += [
        functools.partial(put_lift, flip, way, place)
        for flip in range(2)
        for way in range(2)
        for place in range(PAIRS // 2)
    ]
    for _ in range(UPFRONT):
        spare.pop(0)()
    taps, bias = 0.5 * conv_weight_ref[...], 0.5 * conv_bias_ref[...].reshape(1, MIXED)
    order = chunks(MIXED)
    ready = dot(normal, input_weight_ref[:, E : E + order[0][1]])
    for turn, (start, stop) in enumerate(order):
        mixed = ready
        if turn + 1 < len(order):
            ready = dot(normal, input_weight_ref[:, E + stop : E + order[turn + 1][1]])
        for flip in range(2):
            rows = mixed[flip * BLOCK : (flip + 1) * BLOCK]
            edge_ref[flip, :EDGE, start:stop] = rows[:EDGE]
            edge_ref[flip, EDGE:, start:stop] = rows[BLOCK - EDGE :]
            for tile in range(start // 128, stop // 128):
                lanes = lanes_of(tile)
                place = extended_ref.at[flip, tile]
                place[:PAD] = jnp.zeros((PAD, 128), F32)
                place[PAD + BLOCK :] = jnp.zeros((PAD, 128), F32)
                place[PAD : PAD + BLOCK] = rows[:, tile * 128 - start : tile * 128 - start + 128]
        for flip in range(2):
            for tile in range(start // 128, stop // 128):
                lanes = lanes_of(tile)
                place = extended_ref.at[flip, tile]
                for way in range(2):
                    if spare:
                        spare.pop(0)()
                    half = filtered(place, PAD, lanes, taps, bias, way == 1)
                    activated_ref[2 * flip + way, :, lanes] = half_silu(half).astype(BF16)
    order = chunks(E)
    ready = dot(normal, input_weight_ref[:, : order[0][1]])
    for turn, (start, stop) in enumerate(order):
        gate = ready
        if turn + 1 < len(order):
            ready = dot(normal, input_weight_ref[:, stop : order[turn + 1][1]])
        for _ in range(2):
            if spare:
                spare.pop(0)()
        gate = half_silu(0.5 * gate)
        for flip in range(2):
            silu_gate_ref[flip, :, start:stop] = gate[flip * BLOCK : (flip + 1) * BLOCK]
    for left_over in spare:
        left_over()


def chain_rows(mask, index, block, gain, swap):
    row, column = iota((BLOCK, BLOCK), 0), iota((BLOCK, BLOCK), 1)
    order = jnp.where((index ^ mask) < index, row, 127 - row) == column
    return both_normed(dot(order.astype(BF16), block), gain, swap)


def ahead_kernel(
    mask,
    block_ref,
    norm_gain_ref,
    input_weight_ref,
    step_weight_ref,
    conv_weight_ref,
    conv_bias_ref,
    step_bias_ref,
    log_rate_ref,
    activated_ref,
    edge_ref,
    log_decay_ref,
    extended_ref,
):
    index = lax.axis_index("seq")
    normal = jnp.concatenate(
        chain_rows(mask, index, block_ref[...], norm_gain_ref[...], reversal()), axis=0
    )
    log_decay_ref[...] = log_decays(
        dot_rows(step_weight_ref[...], normal), step_bias_ref[...], log_rate_ref[...]
    )
    taps, bias = 0.5 * conv_weight_ref[...], 0.5 * conv_bias_ref[...].reshape(1, MIXED)
    order = chunks(MIXED)
    ready = dot(normal, input_weight_ref[:, E : E + order[0][1]])
    for turn, (start, stop) in enumerate(order):
        mixed = ready
        if turn + 1 < len(order):
            ready = dot(normal, input_weight_ref[:, E + stop : E + order[turn + 1][1]])
        for flip in range(2):
            rows = mixed[flip * BLOCK : (flip + 1) * BLOCK]
            edge_ref[flip, :EDGE, start:stop] = rows[:EDGE]
            edge_ref[flip, EDGE:, start:stop] = rows[BLOCK - PAD :]
            for tile in range(start // 128, stop // 128):
                lanes = lanes_of(tile)
                place = extended_ref.at[flip, tile]
                place[:PAD] = jnp.zeros((PAD, 128), F32)
                place[PAD:] = rows[:, tile * 128 - start : tile * 128 - start + 128]
                half = filtered(place, PAD, lanes, taps, bias)
                activated_ref[flip, :, lanes] = half_silu(half).astype(BF16)


def join_kernel(count, early, *refs):
    others = [mask for mask in range(1, count) if mask not in early]
    received, refs = refs[: len(others)], refs[len(others) :]
    (
        norm_gain_ref,
        input_weight_ref,
        step_weight_ref,
        conv_weight_ref,
        conv_bias_ref,
        step_bias_ref,
        log_rate_ref,
        skip_gain_ref,
        gate_gain_ref,
        output_weight_ref,
        decay_ref,
        lift_ref,
        activated_ref,
        edge_ref,
        silu_gate_ref,
        *ahead_refs,
        out_ref,
        normal_ref,
        extended_ref,
        memory_ref,
        window_ref,
        patch_ref,
        gated_ref,
    ) = refs
    ahead = {mask: ahead_refs[3 * at : 3 * at + 3] for at, mask in enumerate(early)}
    index = lax.axis_index("seq")
    swap = reversal()
    row, column = iota((BLOCK, BLOCK), 0), iota((BLOCK, BLOCK), 1)
    lower, upper = row >= column, row <= column
    left, right = (column < N).astype(BF16), (column >= N).astype(BF16)
    taps, bias = 0.5 * conv_weight_ref[...], 0.5 * conv_bias_ref[...].reshape(1, MIXED)

    def picked(rows, block):
        result = jnp.zeros((PAD, rows[early[0]].shape[1]), F32)
        for mask, part in rows.items():
            result = jnp.where((index ^ mask) == block, part, result)
        return result

    for place, mask in enumerate(others):
        block = received[place][...]
        for flip, part in enumerate(chain_rows(mask, index, block, norm_gain_ref[...], swap)):
            low = (2 * place + flip) * BLOCK
            normal_ref[low : low + BLOCK] = part
    normal = normal_ref[...]
    log_decay = log_decays(
        dot_rows(step_weight_ref[...], normal), step_bias_ref[...], log_rate_ref[...]
    )
    pieces = {}
    for flip in range(2):
        for place, mask in enumerate(others):
            low = (2 * place + flip) * BLOCK
            pieces[mask, flip] = log_decay[:, low : low + BLOCK]
        for mask in early:
            pieces[mask, flip] = ahead[mask][2][:, flip * BLOCK : (flip + 1) * BLOCK]
    parts = [(mask, flip) for mask in range(1, count) for flip in range(2)]
    tails = exact_dot(
        jnp.concatenate([pieces[part] for part in parts], axis=0), (row > column).astype(BF16)
    )
    wholes = {part: jnp.sum(pieces[part], axis=1, keepdims=True) for part in parts}
    faded = [[], []]
    for at, (mask, flip) in enumerate(parts):
        tail = tails[at * HEADS : (at + 1) * HEADS]
        block = index ^ mask
        for other in range(1, count):
            if other != mask:
                between = index ^ other
                later = ((block < between) & (between < index)) | (
                    (index < between) & (between < block)
                )
                tail = tail + jnp.where(later, wholes[other, flip], 0.0)
        faded[flip].append(jnp.exp(tail))
    faded = [jnp.concatenate(rows, axis=1).astype(BF16) for rows in faded]
    fours = selectors(1, 4)

    writers = [None, None]
    order = chunks(MIXED)
    order = order[-1:] + order[:-1]

    def project(place):
        start, stop = order[place]
        return dot(normal, input_weight_ref[:, E + start : E + stop])

    def fade_of(place, flip):
        return dot_columns(faded[flip], fours[order[place][0] // 256]).astype(BF16)

    ready, coming = project(0), None
    for turn, (start, stop) in enumerate(order):
        mixed = ready
        if turn + 1 < len(order):
            ready = project(turn + 1)
            fades, coming = coming, [fade_of(turn + 1, flip) for flip in range(2)]
        else:
            fades = coming
        for flip in range(2):
            acted = {}
            last = {mask: ahead[mask][1][flip, EDGE:, start:stop] for mask in early}
            for place, mask in enumerate(others):
                low = (2 * place + flip) * BLOCK
                last[mask] = mixed[low + BLOCK - PAD : low + BLOCK]
            window_ref[2 * flip, :PAD, start:stop] = picked(last, index - 1)
            behind = picked(last, index + 1)
            for step in range(K - 1):
                spot = slice(EDGE + step, EDGE + step + 1)
                window_ref[2 * flip + 1, spot, start:stop] = behind[PAD - 1 - step : PAD - step]
            for mask in range(1, count):
                block = index ^ mask
                halo = picked(last, jnp.where(block < index, block - 1, block + 1))
                if mask in ahead:
                    near = []
                    ahead_ref, ahead_edge_ref, _ = ahead[mask]
                    for tile in range(start // 128, stop // 128):
                        lanes = lanes_of(tile)
                        spot = patch_ref.at[2 * early.index(mask) + flip, tile]
                        spot[:PAD] = halo[:, tile * 128 - start : tile * 128 - start + 128]
                        spot[PAD:] = ahead_edge_ref[flip, :EDGE, lanes]
                        half = filtered(spot, PAD, lanes, taps, bias, False, EDGE)
                        patch = half_silu(half).astype(BF16)
                        near.append(
                            jnp.concatenate([patch, ahead_ref[flip, EDGE:, lanes]], axis=0)
                        )
                    acted[mask] = jnp.concatenate(near, axis=1)
                    continue
                place = others.index(mask)
                low = (2 * place + flip) * BLOCK
                near = []
                for tile in range(start // 128, stop // 128):
                    at = tile * 128 - start
                    spot = extended_ref.at[2 * place + flip, tile]
                    spot[:PAD] = halo[:, at : at + 128]
                    spot[PAD:] = mixed[low : low + BLOCK, at : at + 128]
                    half = filtered(spot, PAD, lanes_of(tile), taps, bias)
                    near.append(half_silu(half).astype(BF16))
                acted[mask] = jnp.concatenate(near, axis=1)
            if start == E:
                sides = []
                for mask in range(1, count):
                    maps = acted[mask].T[:N]
                    earlier = jnp.where((index ^ mask) < index, 1.0, 0.0).astype(BF16)
                    later = jnp.where((index ^ mask) < index, 0.0, 1.0).astype(BF16)
                    sides.append(jnp.concatenate([maps * earlier, maps * later], axis=0))
                writers[flip] = jnp.concatenate(sides, axis=1)
                continue
            fade = fades[flip]
            decayed = [
                fade[at * BLOCK : (at + 1) * BLOCK] * acted[at + 1]
                for at in range(count - 1)
            ]
            memory = dot(writers[flip], jnp.concatenate(decayed, axis=0))
            for way in range(2):
                kept = memory[way * N : (way + 1) * N]
                even = (iota(kept.shape, 1) & N) == 0
                chain = 2 * flip + way
                memory_ref[chain, :N, start:stop] = jnp.where(even, kept, 0.0).astype(BF16)
                memory_ref[chain, N:, start:stop] = jnp.where(even, 0.0, kept).astype(BF16)

    skip = wide_row(skip_gain_ref[...])
    for flip in range(2):
        for way in range(2):
            chain = 2 * flip + way
            spot = window_ref.at[chain]
            if way == 0:
                spot[PAD:] = edge_ref[flip, :EDGE]
            else:
                spot[:EDGE] = edge_ref[flip, EDGE:]
            at = PAD if way == 0 else 0
            half = filtered(spot, at, slice(0, MIXED), taps, bias, way == 1, EDGE)
            patch = half_silu(half).astype(BF16)

            def acted(tile):
                lanes = lanes_of(tile)
                if way == 0:
                    near = [patch[:, lanes], activated_ref[chain, EDGE:, lanes]]
                else:
                    near = [activated_ref[chain, : BLOCK - EDGE, lanes], patch[:, lanes]]
                return jnp.concatenate(near, axis=0)

            maps = acted(PAIRS)
            writer, reader = maps[:, :N], maps[:, N:]
            scores = jnp.where(lower if way == 0 else upper, dot_rows(reader, writer), 0.0)
            scores = scores.astype(BF16)
            squares = jnp.zeros((BLOCK, 128), F32)
            doubled = jnp.concatenate([reader, reader], axis=1)
            for pair in range(PAIRS):
                lanes = lanes_of(pair)
                signal = acted(pair)
                signals = jnp.concatenate(
                    [signal * left, signal * right, memory_ref[chain, :, lanes]], axis=0
                )
                weights = jnp.concatenate(
                    [
                        decay_ref[flip, 2 * pair + near] * scores
                        for near in range(2)
                    ]
                    + [lift_ref[chain, :, lanes] * doubled],
                    axis=1,
                )
                inside = dot(weights, signals)
                gated = inside + skip[:, lanes] * signal.astype(F32)
                gated = gated * silu_gate_ref[flip, :, lanes]
                squares = squares + gated * gated
                gated_ref[chain, :, lanes] = gated
            scale = lax.rsqrt(jnp.sum(squares, axis=1, keepdims=True) * (1.0 / E) + eps)
            for pair in range(PAIRS):
                lanes = lanes_of(pair)
                gated_ref[chain, :, lanes] = (
                    gated_ref[chain, :, lanes] * scale * gate_gain_ref[:, lanes]
                )

    normed = gated_ref[...].astype(BF16).reshape(4 * BLOCK, E)
    made = dot(normed, output_weight_ref[...])
    straight, crossed = made[: 2 * BLOCK], made[2 * BLOCK :]
    high, low = split(crossed, 2)
    both = straight + flip_lanes(high, swap) + flip_lanes(low, swap)
    backward = both[BLOCK:].astype(BF16).astype(F32)
    out_ref[...] = (both[:BLOCK] + backward).astype(BF16)


def wide_row(row):
    select = (iota((HEADS, E), 1) // N == iota((HEADS, E), 0)).astype(BF16)
    return exact_dot(jnp.broadcast_to(row, (8, HEADS)), select)[:1]


def swapped(rows, step, count):
    return lax.ppermute(rows, "seq", [(i, i ^ step) for i in range(count)])


def on_device(
    hidden,
    norm_gain,
    input_weight,
    step_weight,
    conv_weight,
    conv_bias,
    step_bias,
    log_rate,
    skip_gain,
    gate_gain,
    output_weight,
):
    count = lax.axis_size("seq")
    top = count // 2
    row = lambda vector: vector.reshape(1, -1)
    whole = pl.BlockSpec(memory_space=pltpu.VMEM)
    shape = jax.ShapeDtypeStruct
    gain, step_map = row(norm_gain), step_weight.T
    step_bias, log_rate = row(step_bias), row(log_rate)
    across = swapped(hidden, top, count)
    first = pl.pallas_call(
        lambda out_ref: out_ref.__setitem__(..., jnp.zeros((8, 128), F32)),
        out_shape=shape((8, 128), F32),
        out_specs=whole,
        compiler_params=pltpu.CompilerParams(vmem_limit_bytes=2**20),
        cost_estimate=pl.CostEstimate(flops=8 * 10**9, bytes_accessed=10**6, transcendentals=0),
        name="opening",
    )()

    def call(kernel, name, outs, scratch, operands, flops, limit, spec=whole):
        return pl.pallas_call(
            kernel,
            out_shape=outs,
            in_specs=[spec] * len(operands),
            out_specs=[whole] * len(outs),
            scratch_shapes=scratch,
            compiler_params=pltpu.CompilerParams(vmem_limit_bytes=limit * 2**20),
            cost_estimate=pl.CostEstimate(
                flops=flops, bytes_accessed=10**7, transcendentals=10**6
            ),
            name=name,
        )(*operands)

    operands = (
        hidden, gain, step_map, step_bias, log_rate, input_weight, conv_weight, conv_bias
    )
    decay, lift, *own = call(
        own_kernel,
        "own_rows",
        [
            shape((2, HEADS, BLOCK, BLOCK), BF16),
            shape((4, BLOCK, E), BF16),
            shape((4, BLOCK, MIXED), BF16),
            shape((2, 2 * EDGE, MIXED), F32),
            shape((2, BLOCK, E), F32),
        ],
        [pltpu.VMEM((2, TILES, BLOCK + 2 * PAD, 128), F32)],
        [first, *operands],
        2 * 10**9,
        16,
    )
    shared = [gain, input_weight, step_map, conv_weight, conv_bias, step_bias, log_rate]

    def ahead(mask, block):
        return call(
            functools.partial(ahead_kernel, mask),
            "ahead_rows",
            [
                shape((2, BLOCK, MIXED), BF16),
                shape((2, EDGE + PAD, MIXED), F32),
                shape((HEADS, 2 * BLOCK), F32),
            ],
            [pltpu.VMEM((2, TILES, PAD + BLOCK, 128), F32)],
            [block, *shared],
            10**9,
            12,
        )

    done, received = {}, {0: hidden}
    if top > 1:
        received[1] = swapped(hidden, 1, count)
        done[1] = ahead(1, received[1])
    across, decay, lift, own, done = lax.optimization_barrier((across, decay, lift, own, done))
    received[top] = across
    for bit in reversed(range(top.bit_length() - 1)):
        for mask in sorted(received):
            if not mask & ((2 << bit) - 1) and mask | 1 << bit not in received:
                received[mask | 1 << bit] = swapped(received[mask], 1 << bit, count)
    done[top] = ahead(top, across)
    others = [mask for mask in range(1, count) if mask not in done]
    (out,) = call(
        functools.partial(join_kernel, count, sorted(done)),
        "join_blocks",
        [shape((BLOCK, EMBED), BF16)],
        [
            pltpu.VMEM((2 * len(others) * BLOCK, EMBED), BF16),
            pltpu.VMEM((2 * len(others), TILES, PAD + BLOCK, 128), F32),
            pltpu.VMEM((4, 2 * N, E), BF16),
            pltpu.VMEM((4, PAD + EDGE, MIXED), F32),
            pltpu.VMEM((2 * len(done), TILES, PAD + EDGE, 128), F32),
            pltpu.VMEM((4, BLOCK, E), F32),
        ],
        [
            *[received[mask] for mask in others],
            *shared,
            row(skip_gain),
            row(gate_gain),
            output_weight,
            decay,
            lift,
            *own,
            *[part for mask in sorted(done) for part in done[mask]],
        ],
        2 * 10**9,
        18 + 2 * len(others),
    )
    return out


def solution(mesh):
    in_specs = (P(("batch", "seq"), None), P(), P(), P(), P(), P(), P(), P(), P(), P(), P())
    out_specs = P(("batch", "seq"), None)
    return jax.shard_map(
        on_device, mesh=mesh, in_specs=in_specs, out_specs=out_specs, check_vma=False
    )
```
